256 devices in a mesh: blk: 64 (over y, x, z_hi), grp: 4 (over z_lo, core).
Axes of the slice: x: 4, y: 4, z: 8 (z_hi: 4, z_lo: 2; z = z_hi * 2 + z_lo), core: 2. Of those that a mesh axis runs over, the one named last changes fastest.
Arguments:
- embeddings: bfloat16 [131072, 1024], P(('blk', 'grp')), may hold values from -1 to 1, as said below
- partners: int32 [3, 64], replicated, may hold values from 0 to 63, as said below
Outputs:
- density: float32 [131072], P(('blk', 'grp'))
The draws below stay inside these ranges and needn't reach their ends.
Inputs may be any that keep to these rules, and one draw needn't show every extreme that they name: Each row of partners pairs the 64 groups: partners[r, partners[r, g]] = g and partners[r, g] != g; no two rounds pair the same two groups. `embeddings`: every row has squared norm 1 up to bfloat16 rounding.
All inputs are finite; a program needn't handle non-finite values.
Results may differ from the reference program's by a relative error of at most 0.0003.
Values may be sent and summed in bfloat16 or wider, within the bound.
A program may use at most 64 MiB of HBM per device.

```python
import math
import jax
import jax.numpy as jnp
from jax import lax

D = 1024
ROUNDS = 3
TOURNEY_GROUPS = 64
GROUP = 2048
ROWS = 131072


def pairing(key):
    key = jax.random.fold_in(key, 11)
    key_labels, key_rounds = jax.random.split(key)
    labels = jax.random.permutation(key_labels, TOURNEY_GROUPS).astype(jnp.int32)
    rounds_drawn = jax.random.permutation(key_rounds, TOURNEY_GROUPS - 1)[:ROUNDS].astype(jnp.int32)
    player = jnp.arange(TOURNEY_GROUPS - 1, dtype=jnp.int32)

    def one_round(turn_value):
        opponent = (2 * turn_value - player) % (TOURNEY_GROUPS - 1)
        opponent = jnp.where(player == turn_value, TOURNEY_GROUPS - 1, opponent).astype(jnp.int32)
        pairing_row = jnp.concatenate([opponent, turn_value[None]]).astype(jnp.int32)
        return jnp.zeros((TOURNEY_GROUPS,), jnp.int32).at[labels].set(labels[pairing_row])
    return jax.vmap(one_round)(rounds_drawn).astype(jnp.int32)


def draw_partners(key, part):
    return pairing(key)


def draw_embeddings(key, part):
    plan = pairing(key)
    key = jax.random.fold_in(key, 5)
    keys = jax.random.split(key, 10)
    key_kind, key_first, key_second, key_centre = (keys[0], keys[1], keys[2], keys[3])
    topic_key, key_theme_of, key_common, key_jitter = (keys[4], keys[5], keys[6], keys[7])
    key_weight, key_scale = (keys[8], keys[9])
    cluster_count = max(GROUP // 16, 2)
    topic_count = 16
    group_ids = jnp.arange(TOURNEY_GROUPS, dtype=jnp.int32)
    slot_kind = jax.random.randint(key_kind, (TOURNEY_GROUPS, GROUP), 0, ROUNDS + 1).astype(jnp.int32)
    first_pick = jax.random.randint(key_first, (TOURNEY_GROUPS, GROUP), 0, cluster_count).astype(jnp.int32)
    second_pick = jax.random.randint(key_second, (TOURNEY_GROUPS, GROUP), 0, cluster_count).astype(jnp.int32)
    pick_index = jnp.minimum(first_pick, second_pick)
    opponent = plan[jnp.minimum(slot_kind, ROUNDS - 1), group_ids[:, None]]
    low_group = jnp.minimum(group_ids[:, None], opponent)
    pair_cluster = (low_group * ROUNDS + slot_kind) * cluster_count + pick_index
    own_cluster = TOURNEY_GROUPS * ROUNDS * cluster_count + group_ids[:, None] * cluster_count + pick_index
    cluster_id = jnp.where(slot_kind < ROUNDS, pair_cluster, own_cluster).astype(jnp.int32).reshape(-1)

    def centre_of(cluster_value):
        return jax.random.normal(jax.random.fold_in(key_centre, cluster_value), (D,), jnp.float32)

    def theme_index(cluster_value):
        return jax.random.randint(jax.random.fold_in(key_theme_of, cluster_value), (), 0, topic_count).astype(jnp.int32)
    centres = jax.vmap(centre_of)(cluster_id)
    theme_ids = jax.vmap(theme_index)(cluster_id)
    themes = jax.random.normal(topic_key, (topic_count, D), jnp.float32)
    common = jax.random.normal(key_common, (D,), jnp.float32)
    jitter = jax.random.normal(key_jitter, (TOURNEY_GROUPS * GROUP, D), jnp.float32)
    share = jax.random.uniform(key_weight, (TOURNEY_GROUPS * GROUP, 1), jnp.float32, 0.05, 0.4)
    noise = jnp.exp(jax.random.uniform(key_scale, (TOURNEY_GROUPS * GROUP, 1), jnp.float32, math.log(0.01), math.log(0.12)))
    theme_weight = 0.35
    vectors = jnp.sqrt(share) * common[None, :] + math.sqrt(theme_weight) * themes[theme_ids]
    vectors = vectors + 0.5 * centres + jnp.sqrt(noise) * jitter
    vectors = vectors / jnp.sqrt(jnp.sum(vectors * vectors, axis=1, keepdims=True))
    return vectors.astype(jnp.bfloat16)


def setup_inputs(seed: int = 0) -> dict:
    key_of = jax.random.split(jax.random.key(seed), 3)
    embeddings = draw_embeddings(jax.random.fold_in(key_of[2], 71), 0)
    partners = draw_partners(jax.random.fold_in(key_of[2], 71), 0)
    return {"embeddings": embeddings, "partners": partners}


SOFTMAX_HEAT = 0.05


def similarity_sum(members, columns):
    score_values = lax.dot_general(members, columns, (((1,), (1,)), ((), ())), preferred_element_type=jnp.float32)
    return jnp.exp((score_values - 1.0) / SOFTMAX_HEAT)


def reference(embeddings, partners):
    groups = embeddings.reshape(TOURNEY_GROUPS, GROUP, D)
    diagonal_mask = jnp.eye(GROUP, dtype=bool)

    def per_group(group_index):
        members = groups[group_index]
        own_terms = jnp.where(diagonal_mask, jnp.float32(0.0), similarity_sum(members, members))
        running_total = jnp.sum(own_terms, axis=1)
        for turn_index in range(ROUNDS):
            opponent = groups[partners[turn_index, group_index]]
            running_total = running_total + jnp.sum(similarity_sum(members, opponent), axis=1)
        return running_total

    return lax.map(per_group, jnp.arange(TOURNEY_GROUPS, dtype=jnp.int32)).reshape(ROWS)
```

```python
import math

import jax
import jax.numpy as jnp
from jax import lax
from jax.experimental import pallas as pl
from jax.experimental.pallas import tpu as pltpu
from jax.sharding import PartitionSpec as P

MESH = pl.DeviceIdType.MESH
HEAT = 0.05
RATE = math.log2(math.e) / HEAT
GROUPS = 64
ROWS = 512
WIDTH = 1024
TILE = 256


def similarity(columns, members):
    c = lax.dot_general(columns, members, (((1,), (1,)), ((), ())), preferred_element_type=jnp.float32)
    return jnp.exp2(c * RATE - RATE)


def lane_sums(total):
    ones = jnp.ones((8, 128), jnp.float32)
    return lax.dot_general(
        ones, total, (((1,), (1,)), ((), ())),
        precision=lax.Precision.HIGHEST, preferred_element_type=jnp.float32,
    )


def kernel(
    partners, x, out,
    own, pieces, stage1, stage2, met1, met2, own_acc, acc1, acc2, row_acc, row_in, col_out, col_all,
    hop_a, low_a, hop_b, low_b, pick1, pick2,
    line_y, line_z, other, spread_send, spread_recv, send1, recv1, send2, recv2,
    own_send, own_recv, fwd_send, fwd_recv, row_send, row_recv, col_send, col_recv,
):
    blk, grp = lax.axis_index("blk"), lax.axis_index("grp")
    y, xx, h = blk // 16, (blk // 4) % 4, blk % 4
    e, c = grp // 2, grp % 2

    def at(y_, x_, h_, e_=None, c_=None):
        e_ = e if e_ is None else e_
        c_ = c if c_ is None else c_
        return ((y_ % 4) * 16 + (x_ % 4) * 4 + h_ % 4, e_ * 2 + c_)

    def signal(sem, device):
        pl.semaphore_signal(sem, inc=1, device_id=device, device_id_type=MESH)

    def remote(src, dst, send, recv, device):
        return pltpu.make_async_remote_copy(
            src_ref=src, dst_ref=dst, send_sem=send, recv_sem=recv, device_id=device, device_id_type=MESH
        )

    def drain(ref, sem):
        pltpu.make_async_copy(ref, ref, sem).wait()

    barrier = pltpu.get_barrier_semaphore()
    for i in (1, 2, 3):
        signal(barrier, at(y + i, xx, h))
        signal(barrier, at(y, xx + i, h))
        signal(barrier, at(y, xx, h + i))
    signal(barrier, at(y, xx, h, 1 - e))
    signal(barrier, at(y, xx, h, e, 1 - c))
    signal(barrier, at(y, xx, h, 1 - e, 1 - c))
    pl.semaphore_wait(barrier, 12)
    own_core = remote(x, own.at[grp], own_send.at[0], own_recv.at[0], at(y, xx, h, e, 1 - c))
    own_core.start()
    for i in (1, 2, 3):
        signal(line_y, at(y + i, xx, h))
    pl.semaphore_wait(line_y, 3)
    for i in (1, 2, 3):
        signal(line_z, at(y, xx, h + i))
    pl.semaphore_wait(line_z, 3)

    def spread(k, carry):
        ty, tx, th = (y + k // 16) % 4, (xx + (k // 4) % 4) % 4, (h + k) % 4
        row = pl.multiple_of((th * 8 + ty * 2 + tx // 2) * 16, 16)
        col = pl.multiple_of((tx % 2) * 512, 512)
        remote(
            x.at[pl.ds(row, 16), pl.ds(col, 512)], pieces.at[blk], spread_send, spread_recv, at(ty, tx, th)
        ).start()
        return carry

    lax.fori_loop(1, GROUPS, spread, 0)
    my_row = pl.multiple_of((h * 8 + y * 2 + xx // 2) * 16, 16)
    my_col = pl.multiple_of((xx % 2) * 512, 512)
    pieces[blk] = x[pl.ds(my_row, 16), pl.ds(my_col, 512)]

    def mate(g):
        return g + 4 - 8 * ((g // 4) % 2)

    def begin(g, carry):
        hop_a[0, g] = partners[1, partners[0, g]]
        hop_b[0, g] = mate(partners[2, g])
        low_a[g] = g
        low_b[g] = g
        return carry

    lax.fori_loop(0, GROUPS, begin, 0)
    for step in range(5):
        now, later = step % 2, (step + 1) % 2

        def double(g, carry):
            s, t = hop_a[now, g], hop_b[now, g]
            low_a[g] = jnp.minimum(low_a[g], low_a[s])
            low_b[g] = jnp.minimum(low_b[g], low_b[t])
            hop_a[later, g] = hop_a[now, s]
            hop_b[later, g] = hop_b[now, t]
            return carry

        lax.fori_loop(0, GROUPS, double, 0)

    def first(g):
        return low_a[g] < low_a[partners[0, g]]

    def receives(g):
        return low_b[g] < low_b[partners[2, g]]

    def choose(g, carry):
        pick1[g] = jnp.where(first(g), partners[0, g], partners[1, g])
        pick2[g] = partners[2, jnp.where(receives(g), g, mate(g))]
        return carry

    lax.fori_loop(0, GROUPS, choose, 0)

    own_acc[...] = jnp.zeros_like(own_acc)
    diagonal = lax.broadcasted_iota(jnp.int32, (ROWS, TILE), 0)
    across = lax.broadcasted_iota(jnp.int32, (ROWS, TILE), 1)

    def own_tile(t, carry):
        start = pl.multiple_of(t * TILE, TILE)
        block = x[pl.ds(start, TILE), :]
        own[grp, pl.ds(start, TILE), :] = block
        terms = jnp.where(diagonal == across + t * TILE, 0.0, similarity(x[...], block))
        own_acc[...] += terms[:, :128] + terms[:, 128:]
        return carry

    lax.fori_loop(0, ROWS // TILE, own_tile, 0)

    def own_others(member):
        def tile(t, carry):
            terms = similarity(x[...], own[member, pl.ds(pl.multiple_of(t * TILE, TILE), TILE), :])
            own_acc[...] += terms[:, :128] + terms[:, 128:]
            return carry

        lax.fori_loop(0, ROWS // TILE, tile, 0)

    own_core.wait()
    own_others(e * 2 + 1 - c)

    drain(pieces.at[pl.ds(0, GROUPS - 1)], spread_recv)
    signal(other, at(y, xx, h, 1 - e))
    pl.semaphore_wait(other, 1)
    own_chip = remote(x, own.at[grp], own_send.at[1], own_recv.at[1], at(y, xx, h, 1 - e))
    own_chip.start()

    def place(k):
        d = k % 4
        ty, tx, th = (y + k // 16) % 4, (xx + (k // 4) % 4) % 4, (h + k) % 4
        to = jnp.where(d == 0, e, jnp.where(d == 1, 0, jnp.where(d == 3, 1, 1 - e)))
        second0 = jnp.where(e == 0, d, d - 1)
        second1 = jnp.where(e == 0, 3 - d, jnp.where(d == 0, 0, 1))
        slot = 2 * e + jnp.where(to == 0, second0, second1)
        row = pl.multiple_of(slot * 128 + (y * 2 + xx // 2) * 16, 16)
        return ty, tx, th, to, row

    def half_units(k, carry):
        ty, tx, th, to, row = place(k)
        lane = pl.multiple_of((tx % 2) * 256, 256)
        stage2[k] = pieces[pick2[ty * 16 + tx * 4 + th], :, pl.ds(lane, 256)]
        col = pl.multiple_of((xx % 2) * 512 + (tx % 2) * 256, 256)
        remote(
            stage2.at[k], met2.at[pl.ds(row, 16), pl.ds(col, 256)], send2, recv2, at(ty, tx, th, to)
        ).start()
        return carry

    def units(k, carry):
        ty, tx, th, to, row = place(k)
        stage1[k] = pieces[pick1[ty * 16 + tx * 4 + th]]
        remote(
            stage1.at[k], met1.at[pl.ds(row, 16), pl.ds(my_col, 512)], send1, recv1, at(ty, tx, th, to)
        ).start()
        return carry

    lax.fori_loop(1, GROUPS, half_units, 0)
    lax.fori_loop(1, GROUPS, units, 0)
    home = pl.multiple_of((2 * e + 0) * 128 + (y * 2 + xx // 2) * 16, 16)
    half = pl.multiple_of((xx % 2) * 256, 256)
    met1[pl.ds(home, 16), pl.ds(my_col, 512)] = pieces[pick1[blk]]
    met2[pl.ds(home, 16), pl.ds(pl.multiple_of(my_col + half, 256), 256)] = pieces[
        pick2[blk], :, pl.ds(half, 256)
    ]

    own_chip.wait()
    across_core = remote(
        own.at[2 - 2 * e + c], own.at[2 - 2 * e + c], own_send.at[2], own_recv.at[2], at(y, xx, h, e, 1 - c)
    )
    across_core.start()
    own_others(2 - 2 * e + c)
    across_core.wait()
    own_others(2 - 2 * e + 1 - c)

    def meet(met, acc, counts):
        acc[...] = jnp.zeros_like(acc)

        def tile(t, carry):
            member, part = t // 2, pl.multiple_of((t % 2) * TILE, TILE)
            terms = similarity(met[...], own[member, pl.ds(part, TILE), :])
            acc[...] += terms[:, :128] + terms[:, 128:]
            sums = jnp.sum(terms.reshape(ROWS // 8, 8, TILE), axis=0)
            if counts is not None:
                row_acc[member, :, pl.ds(part, TILE)] = jnp.where(counts, sums, 0.0)
            else:
                row_acc[member, :, pl.ds(part, TILE)] += sums
            return carry

        lax.fori_loop(0, 4 * ROWS // TILE, tile, 0)

    drain(stage2.at[pl.ds(0, GROUPS - 1)], recv2)
    pair = at(y, xx + 1 - 2 * (xx % 2), h)
    for i in range(2):
        columns = pl.ds(pl.multiple_of(i * 512 + half, 256), 256)
        remote(met2.at[:, columns], met2.at[:, columns], fwd_send.at[i], fwd_recv.at[i], pair).start()
    for i in range(2):
        columns = pl.ds(pl.multiple_of(i * 512 + half, 256), 256)
        remote(met2.at[:, columns], met2.at[:, columns], fwd_send.at[i], fwd_recv.at[i], pair).wait()
    meet(met2, acc2, receives(blk))

    drain(stage1.at[pl.ds(0, GROUPS - 1)], recv1)
    meet(met1, acc1, None)

    siblings = []
    for i in (1, 2, 3):
        member = (grp + i) % 4
        copy = remote(
            row_acc.at[member], row_in.at[i - 1], row_send.at[i - 1], row_recv.at[i - 1], (blk, member)
        )
        copy.start()
        siblings.append(copy)
    for u, acc in ((0, acc1), (1, acc2)):
        sums = lane_sums(acc[...])
        for s in range(4):
            col_out[s // 2, u * 2 + s % 2, :] = sums[0, s * 128 : (s + 1) * 128]
    line = []
    for i in range(1, 8):
        th, te = (h + i // 2) % 4, (e + i) % 2
        copy = remote(
            col_out.at[te], col_all.at[xx, y, 2 * h + e], col_send.at[0], col_recv.at[0], at(y, xx, th, te)
        )
        copy.start()
    col_all[xx, y, 2 * h + e] = col_out[e]
    own_sums = lane_sums(own_acc[...])[0:1, :]
    drain(col_all.at[0, 0, pl.ds(0, 7)], col_recv.at[0])
    for i in (1, 2, 3):
        remote(
            col_all.at[xx, y], col_all.at[xx, y], col_send.at[1], col_recv.at[1], at(y + i, xx, h)
        ).start()
    for copy in siblings:
        copy.wait()
    total = row_acc[grp] + row_in[0] + row_in[1] + row_in[2]
    density = jnp.sum(total, axis=0, keepdims=True) + own_sums
    drain(col_all.at[0, pl.ds(0, 3)], col_recv.at[1])
    for i in (1, 2, 3):
        remote(col_all.at[xx], col_all.at[xx], col_send.at[2], col_recv.at[2], at(y, xx + i, h)).start()
    drain(col_all.at[pl.ds(0, 3)], col_recv.at[2])

    a1 = jnp.where(first(blk), partners[1, blk], partners[0, blk])
    a2 = partners[2, blk]
    silent = jnp.logical_not(receives(blk))

    def column_sums(a, u, q):
        ay, ax, ah = a // 16, (a // 4) % 4, a % 4
        d = (ah - q + 4) % 4
        j0 = jnp.where(d == 2, 3, jnp.where(d == 3, 2, d))
        j1 = jnp.where(d == 0, 2, jnp.where(d == 3, 3, d - 1))
        j = jnp.where(e == 0, j0, j1)
        return col_all[ax, ay, 2 * ah + j // 2, pl.ds(u * 2 + j % 2, 1), :]

    for q in range(4):
        part = density[:, q * 128 : (q + 1) * 128] + column_sums(a1, 0, q)
        part = part + jnp.where(silent, column_sums(a2, 1, q), 0.0)
        out[pl.ds(q, 1), :] = part

    drain(pieces.at[pl.ds(0, GROUPS - 1)], spread_send)
    drain(stage1.at[pl.ds(0, GROUPS - 1)], send1)
    drain(stage2.at[pl.ds(0, GROUPS - 1)], send2)
    drain(col_all.at[0, 0, pl.ds(0, 7)], col_send.at[0])
    drain(col_all.at[0, pl.ds(0, 3)], col_send.at[1])
    drain(col_all.at[pl.ds(0, 3)], col_send.at[2])


def body(embeddings, partners):
    f32, bf16, dma = jnp.float32, jnp.bfloat16, pltpu.SemaphoreType.DMA
    regular = pltpu.SemaphoreType.REGULAR
    density = pl.pallas_call(
        kernel,
        out_shape=jax.ShapeDtypeStruct((4, 128), f32),
        in_specs=[
            pl.BlockSpec(memory_space=pltpu.SMEM),
            pl.BlockSpec(memory_space=pltpu.VMEM),
        ],
        out_specs=pl.BlockSpec(memory_space=pltpu.VMEM),
        scratch_shapes=[
            pltpu.VMEM((4, ROWS, WIDTH), bf16),
            pltpu.VMEM((GROUPS, 16, 512), bf16),
            pltpu.VMEM((GROUPS, 16, 512), bf16),
            pltpu.VMEM((GROUPS, 16, 256), bf16),
            pltpu.VMEM((ROWS, WIDTH), bf16),
            pltpu.VMEM((ROWS, WIDTH), bf16),
            pltpu.VMEM((ROWS, 128), f32),
            pltpu.VMEM((ROWS, 128), f32),
            pltpu.VMEM((ROWS, 128), f32),
            pltpu.VMEM((4, 8, ROWS), f32),
            pltpu.VMEM((3, 8, ROWS), f32),
            pltpu.VMEM((2, 4, 128), f32),
            pltpu.VMEM((4, 4, 8, 4, 128), f32),
            pltpu.SMEM((2, GROUPS), jnp.int32),
            pltpu.SMEM((GROUPS,), jnp.int32),
            pltpu.SMEM((2, GROUPS), jnp.int32),
            pltpu.SMEM((GROUPS,), jnp.int32),
            pltpu.SMEM((GROUPS,), jnp.int32),
            pltpu.SMEM((GROUPS,), jnp.int32),
            regular, regular, regular,
            dma, dma, dma, dma, dma, dma,
            dma((3,)), dma((3,)), dma((2,)), dma((2,)), dma((3,)), dma((3,)), dma((3,)), dma((3,)),
        ],
        compiler_params=pltpu.CompilerParams(
            collective_id=0, has_side_effects=True, vmem_limit_bytes=40 * 2**20
        ),
        cost_estimate=pl.CostEstimate(
            flops=2 * 4 * ROWS * 3 * ROWS * WIDTH, bytes_accessed=2**20, transcendentals=12 * ROWS * ROWS
        ),
    )(partners, embeddings)
    return density.reshape(ROWS)


def solution(mesh):
    return jax.shard_map(
        body,
        mesh=mesh,
        in_specs=(P(("blk", "grp"), None), P()),
        out_specs=P(("blk", "grp")),
        check_vma=False,
    )
```

```python
import math

import jax
import jax.numpy as jnp
from jax import lax
from jax.experimental import pallas as pl
from jax.experimental.pallas import tpu as pltpu
from jax.sharding import PartitionSpec as P

MESH = pl.DeviceIdType.MESH
HEAT = 0.05
RATE = math.log2(math.e) / HEAT
GROUPS = 64
ROWS = 512
WIDTH = 1024
TILE = 256


def similarity(columns, members):
    c = lax.dot_general(columns, members, (((1,), (1,)), ((), ())), preferred_element_type=jnp.float32)
    return jnp.exp2(c * RATE - RATE)


def lane_sums(total):
    ones = jnp.ones((8, 128), jnp.float32)
    return lax.dot_general(
        ones, total, (((1,), (1,)), ((), ())),
        precision=lax.Precision.HIGHEST, preferred_element_type=jnp.float32,
    )


def kernel(
    rounds, rows, out,
    own, pieces, stage1, stage2, met1, met2, own_acc, acc1, acc2, row_acc, row_in, col_out, col_all,
    partners, hop_a, low_a, hop_b, low_b, pick1, pick2,
    line_y, line_z, other, spread_send, spread_recv, send1, recv1, send2, recv2,
    load, table, own_send, own_recv, fwd_send, fwd_recv, row_send, row_recv, col_send, col_recv,
):
    blk, grp = lax.axis_index("blk"), lax.axis_index("grp")
    y, xx, h = blk // 16, (blk // 4) % 4, blk % 4
    e, c = grp // 2, grp % 2

    def at(y_, x_, h_, e_=None, c_=None):
        e_ = e if e_ is None else e_
        c_ = c if c_ is None else c_
        return ((y_ % 4) * 16 + (x_ % 4) * 4 + h_ % 4, e_ * 2 + c_)

    def signal(sem, device):
        pl.semaphore_signal(sem, inc=1, device_id=device, device_id_type=MESH)

    def remote(src, dst, send, recv, device):
        return pltpu.make_async_remote_copy(
            src_ref=src, dst_ref=dst, send_sem=send, recv_sem=recv, device_id=device, device_id_type=MESH
        )

    def drain(ref, sem):
        pltpu.make_async_copy(ref, ref, sem).wait()

    x = own.at[grp]
    fetch = pltpu.make_async_copy(rows, x, load)
    fetch.start()
    fetch_table = pltpu.make_async_copy(rounds, partners, table)
    fetch_table.start()

    def spread(dy, dx, dh):
        ty, tx, th = (y + dy) % 4, (xx + dx) % 4, (h + dh) % 4
        row = pl.multiple_of((th * 8 + ty * 2 + tx // 2) * 16, 16)
        col = pl.multiple_of((tx % 2) * 512, 512)
        remote(
            x.at[pl.ds(row, 16), pl.ds(col, 512)], pieces.at[blk], spread_send, spread_recv, at(ty, tx, th)
        ).start()

    def spread_plane(j, carry):
        spread(1 + j // 3, 1 + j % 3, 0)
        return carry

    def spread_rest(j, carry):
        spread((1 + j // 3) // 4, (1 + j // 3) % 4, 1 + j % 3)
        return carry

    barrier = pltpu.get_barrier_semaphore()
    for i in (1, 2, 3):
        signal(barrier, at(y + i, xx, h))
        signal(barrier, at(y, xx + i, h))
        signal(barrier, at(y, xx, h + i))
    signal(barrier, at(y, xx, h, 1 - e))
    signal(barrier, at(y, xx, h, e, 1 - c))
    signal(barrier, at(y, xx, h, 1 - e, 1 - c))
    fetch.wait()
    pl.semaphore_wait(barrier, 12)
    for i in (1, 2, 3):
        signal(line_y, at(y + i, xx, h))

    def own_chip(i):
        part = own.at[grp, pl.ds(i * TILE, TILE)]
        return remote(part, part, own_send.at[1 + i], own_recv.at[1 + i], at(y, xx, h, 1 - e))

    own_chip(0).start()
    for i in (1, 2, 3):
        spread(0, 0, i)
        spread(i, 0, 0)
        spread(0, i, 0)
    pl.semaphore_wait(line_y, 3)
    for i in (1, 2, 3):
        signal(line_z, at(y, xx, h + i))
    lax.fori_loop(0, 9, spread_plane, 0)
    pl.semaphore_wait(line_z, 3)
    signal(other, at(y, xx, h, 1 - e))
    lax.fori_loop(0, 45, spread_rest, 0)
    own_core = remote(x, x, own_send.at[0], own_recv.at[0], at(y, xx, h, e, 1 - c))
    own_core.start()
    my_row = pl.multiple_of((h * 8 + y * 2 + xx // 2) * 16, 16)
    my_col = pl.multiple_of((xx % 2) * 512, 512)
    pieces[blk] = x[pl.ds(my_row, 16), pl.ds(my_col, 512)]

    def mate(g):
        return g + 4 - 8 * ((g // 4) % 2)

    def begin(g, carry):
        hop_a[0, g] = partners[1, partners[0, g]]
        hop_b[0, g] = mate(partners[2, g])
        low_a[g] = g
        low_b[g] = g
        return carry

    fetch_table.wait()
    lax.fori_loop(0, GROUPS, begin, 0)
    for step in range(5):
        now, later = step % 2, (step + 1) % 2

        def double(g, carry):
            s, t = hop_a[now, g], hop_b[now, g]
            low_a[g] = jnp.minimum(low_a[g], low_a[s])
            low_b[g] = jnp.minimum(low_b[g], low_b[t])
            hop_a[later, g] = hop_a[now, s]
            hop_b[later, g] = hop_b[now, t]
            return carry

        lax.fori_loop(0, GROUPS, double, 0)

    def first(g):
        return low_a[g] < low_a[partners[0, g]]

    def receives(g):
        return low_b[g] < low_b[partners[2, g]]

    def choose(g, carry):
        pick1[g] = jnp.where(first(g), partners[0, g], partners[1, g])
        pick2[g] = partners[2, jnp.where(receives(g), g, mate(g))]
        return carry

    lax.fori_loop(0, GROUPS, choose, 0)

    own_acc[...] = jnp.zeros_like(own_acc)
    diagonal = lax.broadcasted_iota(jnp.int32, (ROWS, TILE), 0)
    across = lax.broadcasted_iota(jnp.int32, (ROWS, TILE), 1)

    for t in range(ROWS // TILE):
        terms = similarity(x[...], x[t * TILE : (t + 1) * TILE, :])
        terms = jnp.where(diagonal == across + t * TILE, 0.0, terms)
        own_acc[...] += terms[:, :128] + terms[:, 128:]

    def own_others(member):
        for t in range(ROWS // TILE):
            terms = similarity(x[...], own[member, t * TILE : (t + 1) * TILE, :])
            own_acc[...] += terms[:, :128] + terms[:, 128:]

    own_core.wait()
    own_others(e * 2 + 1 - c)

    drain(pieces.at[pl.ds(0, GROUPS - 1)], spread_recv)
    pl.semaphore_wait(other, 1)
    own_chip(1).start()

    def place(k):
        d = k % 4
        ty, tx, th = (y + k // 16) % 4, (xx + (k // 4) % 4) % 4, (h + k) % 4
        to = jnp.where(d == 0, e, jnp.where(d == 1, 0, jnp.where(d == 3, 1, 1 - e)))
        second0 = jnp.where(e == 0, d, d - 1)
        second1 = jnp.where(e == 0, 3 - d, jnp.where(d == 0, 0, 1))
        slot = 2 * e + jnp.where(to == 0, second0, second1)
        row = pl.multiple_of(slot * 128 + (y * 2 + xx // 2) * 16, 16)
        return ty, tx, th, to, row

    def half_units(k, carry):
        ty, tx, th, to, row = place(k)
        lane = pl.multiple_of((tx % 2) * 256, 256)
        stage2[k] = pieces[pick2[ty * 16 + tx * 4 + th], :, pl.ds(lane, 256)]
        col = pl.multiple_of((xx % 2) * 512 + (tx % 2) * 256, 256)
        remote(
            stage2.at[k], met2.at[pl.ds(row, 16), pl.ds(col, 256)], send2, recv2, at(ty, tx, th, to)
        ).start()
        return carry

    def units(k, carry):
        ty, tx, th, to, row = place(k)
        stage1[k] = pieces[pick1[ty * 16 + tx * 4 + th]]
        remote(
            stage1.at[k], met1.at[pl.ds(row, 16), pl.ds(my_col, 512)], send1, recv1, at(ty, tx, th, to)
        ).start()
        return carry

    lax.fori_loop(1, GROUPS, half_units, 0)
    lax.fori_loop(1, GROUPS, units, 0)
    home = pl.multiple_of((2 * e + 0) * 128 + (y * 2 + xx // 2) * 16, 16)
    half = pl.multiple_of((xx % 2) * 256, 256)
    met1[pl.ds(home, 16), pl.ds(my_col, 512)] = pieces[pick1[blk]]
    met2[pl.ds(home, 16), pl.ds(pl.multiple_of(my_col + half, 256), 256)] = pieces[
        pick2[blk], :, pl.ds(half, 256)
    ]

    def meet(met, acc, counts):
        acc[...] = jnp.zeros_like(acc)

        for t in range(4 * ROWS // TILE):
            member, part = t // 2, slice((t % 2) * TILE, (t % 2 + 1) * TILE)
            terms = similarity(met[...], own[member, part, :])
            acc[...] += terms[:, :128] + terms[:, 128:]
            sums = jnp.sum(terms.reshape(ROWS // 8, 8, TILE), axis=0)
            if counts is not None:
                row_acc[member, :, part] = jnp.where(counts, sums, 0.0)
            else:
                row_acc[member, :, part] += sums

    drain(stage2.at[pl.ds(0, GROUPS - 1)], recv2)
    pair = at(y, xx + 1 - 2 * (xx % 2), h)
    for i in range(2):
        columns = pl.ds(pl.multiple_of(i * 512 + half, 256), 256)
        remote(met2.at[:, columns], met2.at[:, columns], fwd_send.at[i], fwd_recv.at[i], pair).start()
    own_chip(0).wait()
    own_chip(1).wait()
    across_core = remote(
        own.at[2 - 2 * e + c], own.at[2 - 2 * e + c], own_send.at[3], own_recv.at[3], at(y, xx, h, e, 1 - c)
    )
    across_core.start()
    own_others(2 - 2 * e + c)
    across_core.wait()
    own_others(2 - 2 * e + 1 - c)
    for i in range(2):
        columns = pl.ds(pl.multiple_of(i * 512 + half, 256), 256)
        remote(met2.at[:, columns], met2.at[:, columns], fwd_send.at[i], fwd_recv.at[i], pair).wait()
    meet(met2, acc2, receives(blk))

    drain(stage1.at[pl.ds(0, GROUPS - 1)], recv1)
    meet(met1, acc1, None)

    siblings = []
    for i in (1, 2, 3):
        member = (grp + i) % 4
        copy = remote(
            row_acc.at[member], row_in.at[i - 1], row_send.at[i - 1], row_recv.at[i - 1], (blk, member)
        )
        copy.start()
        siblings.append(copy)
    for u, acc in ((0, acc1), (1, acc2)):
        sums = lane_sums(acc[...])
        for s in range(4):
            col_out[s // 2, u * 2 + s % 2, :] = sums[0, s * 128 : (s + 1) * 128]
    line = []
    for i in range(1, 8):
        th, te = (h + i // 2) % 4, (e + i) % 2
        copy = remote(
            col_out.at[te], col_all.at[xx, y, 2 * h + e], col_send.at[0], col_recv.at[0], at(y, xx, th, te)
        )
        copy.start()
    col_all[xx, y, 2 * h + e] = col_out[e]
    own_sums = lane_sums(own_acc[...])[0:1, :]
    drain(col_all.at[0, 0, pl.ds(0, 7)], col_recv.at[0])
    for i in (1, 2, 3):
        remote(
            col_all.at[xx, y], col_all.at[xx, y], col_send.at[1], col_recv.at[1], at(y + i, xx, h)
        ).start()
    for copy in siblings:
        copy.wait()
    total = row_acc[grp] + row_in[0] + row_in[1] + row_in[2]
    density = jnp.sum(total, axis=0, keepdims=True) + own_sums
    drain(col_all.at[0, pl.ds(0, 3)], col_recv.at[1])
    for i in (1, 2, 3):
        remote(col_all.at[xx], col_all.at[xx], col_send.at[2], col_recv.at[2], at(y, xx + i, h)).start()
    drain(col_all.at[pl.ds(0, 3)], col_recv.at[2])

    a1 = jnp.where(first(blk), partners[1, blk], partners[0, blk])
    a2 = partners[2, blk]
    silent = jnp.logical_not(receives(blk))

    def column_sums(a, u, q):
        ay, ax, ah = a // 16, (a // 4) % 4, a % 4
        d = (ah - q + 4) % 4
        j0 = jnp.where(d == 2, 3, jnp.where(d == 3, 2, d))
        j1 = jnp.where(d == 0, 2, jnp.where(d == 3, 3, d - 1))
        j = jnp.where(e == 0, j0, j1)
        return col_all[ax, ay, 2 * ah + j // 2, pl.ds(u * 2 + j % 2, 1), :]

    for q in range(4):
        part = density[:, q * 128 : (q + 1) * 128] + column_sums(a1, 0, q)
        part = part + jnp.where(silent, column_sums(a2, 1, q), 0.0)
        out[pl.ds(q, 1), :] = part

    drain(pieces.at[pl.ds(0, GROUPS - 1)], spread_send)
    drain(stage1.at[pl.ds(0, GROUPS - 1)], send1)
    drain(stage2.at[pl.ds(0, GROUPS - 1)], send2)
    drain(col_all.at[0, 0, pl.ds(0, 7)], col_send.at[0])
    drain(col_all.at[0, pl.ds(0, 3)], col_send.at[1])
    drain(col_all.at[pl.ds(0, 3)], col_send.at[2])


def body(embeddings, partners):
    f32, bf16, dma = jnp.float32, jnp.bfloat16, pltpu.SemaphoreType.DMA
    regular = pltpu.SemaphoreType.REGULAR
    density = pl.pallas_call(
        kernel,
        out_shape=jax.ShapeDtypeStruct((4, 128), f32),
        in_specs=[
            pl.BlockSpec(memory_space=pl.ANY),
            pl.BlockSpec(memory_space=pl.ANY),
        ],
        out_specs=pl.BlockSpec(memory_space=pltpu.VMEM),
        scratch_shapes=[
            pltpu.VMEM((4, ROWS, WIDTH), bf16),
            pltpu.VMEM((GROUPS, 16, 512), bf16),
            pltpu.VMEM((GROUPS, 16, 512), bf16),
            pltpu.VMEM((GROUPS, 16, 256), bf16),
            pltpu.VMEM((ROWS, WIDTH), bf16),
            pltpu.VMEM((ROWS, WIDTH), bf16),
            pltpu.VMEM((ROWS, 128), f32),
            pltpu.VMEM((ROWS, 128), f32),
            pltpu.VMEM((ROWS, 128), f32),
            pltpu.VMEM((4, 8, ROWS), f32),
            pltpu.VMEM((3, 8, ROWS), f32),
            pltpu.VMEM((2, 4, 128), f32),
            pltpu.VMEM((4, 4, 8, 4, 128), f32),
            pltpu.SMEM((3, GROUPS), jnp.int32),
            pltpu.SMEM((2, GROUPS), jnp.int32),
            pltpu.SMEM((GROUPS,), jnp.int32),
            pltpu.SMEM((2, GROUPS), jnp.int32),
            pltpu.SMEM((GROUPS,), jnp.int32),
            pltpu.SMEM((GROUPS,), jnp.int32),
            pltpu.SMEM((GROUPS,), jnp.int32),
            regular, regular, regular,
            dma, dma, dma, dma, dma, dma,
            dma, dma, dma((4,)), dma((4,)), dma((2,)), dma((2,)), dma((3,)), dma((3,)), dma((3,)), dma((3,)),
        ],
        compiler_params=pltpu.CompilerParams(
            collective_id=0, has_side_effects=True, vmem_limit_bytes=60 * 2**20
        ),
        cost_estimate=pl.CostEstimate(
            flops=2 * 4 * ROWS * 3 * ROWS * WIDTH, bytes_accessed=2**20, transcendentals=12 * ROWS * ROWS
        ),
    )(partners, embeddings)
    return density.reshape(ROWS)


def solution(mesh):
    return jax.shard_map(
        body,
        mesh=mesh,
        in_specs=(P(("blk", "grp"), None), P()),
        out_specs=P(("blk", "grp")),
        check_vma=False,
    )
```

```python
import math

import jax
import jax.numpy as jnp
from jax import lax
from jax.experimental import pallas as pl
from jax.experimental.pallas import tpu as pltpu
from jax.sharding import PartitionSpec as P

MESH = pl.DeviceIdType.MESH
HEAT = 0.05
RATE = math.log2(math.e) / HEAT
GROUPS = 64
ROWS = 512
WIDTH = 1024
TILE = 256
CHUNK = 16
FEW, MANY = 7, 21
EARLY = ROWS - CHUNK * (FEW + MANY)


def similarity(columns, members):
    c = lax.dot_general(columns, members, (((1,), (1,)), ((), ())), preferred_element_type=jnp.float32)
    return jnp.exp2(c * RATE - RATE)


def lane_sums(total):
    ones = jnp.ones((8, 128), jnp.float32)
    return lax.dot_general(
        ones, total, (((1,), (1,)), ((), ())),
        precision=lax.Precision.HIGHEST, preferred_element_type=jnp.float32,
    )


def kernel(
    rounds, rows, out,
    own, pieces, stage1, stage2, met1, met2, own_acc, acc1, acc2, row_acc, row_in, col_out, col_line, col_stage, col_plane,
    partners, hop_a, low_a, hop_b, low_b, pick1, pick2, back,
    line_y, line_z, other, spread_send, spread_recv, send1, recv1, send2, recv2,
    load, table, own_send, own_recv, fwd_send, fwd_recv, row_send, row_recv, col_send, col_recv,
):
    blk, grp = lax.axis_index("blk"), lax.axis_index("grp")
    y, xx, h = blk // 16, (blk // 4) % 4, blk % 4
    e, c = grp // 2, grp % 2

    def at(y_, x_, h_, e_=None, c_=None):
        e_ = e if e_ is None else e_
        c_ = c if c_ is None else c_
        return ((y_ % 4) * 16 + (x_ % 4) * 4 + h_ % 4, e_ * 2 + c_)

    def signal(sem, device):
        pl.semaphore_signal(sem, inc=1, device_id=device, device_id_type=MESH)

    def remote(src, dst, send, recv, device):
        return pltpu.make_async_remote_copy(
            src_ref=src, dst_ref=dst, send_sem=send, recv_sem=recv, device_id=device, device_id_type=MESH
        )

    def drain(ref, sem):
        pltpu.make_async_copy(ref, ref, sem).wait()

    x = own.at[grp]
    fetch = pltpu.make_async_copy(rows, x, load)
    fetch.start()
    fetch_table = pltpu.make_async_copy(rounds, partners, table)
    fetch_table.start()

    def spread(dy, dx, dh):
        ty, tx, th = (y + dy) % 4, (xx + dx) % 4, (h + dh) % 4
        row = pl.multiple_of((th * 8 + ty * 2 + tx // 2) * 16, 16)
        col = pl.multiple_of((tx % 2) * 512, 512)
        remote(
            x.at[pl.ds(row, 16), pl.ds(col, 512)], pieces.at[blk], spread_send, spread_recv, at(ty, tx, th)
        ).start()

    def spread_plane(j, carry):
        spread(1 + j // 3, 1 + j % 3, 0)
        return carry

    def spread_rest(j, carry):
        spread((1 + j // 3) // 4, (1 + j // 3) % 4, 1 + j % 3)
        return carry

    barrier = pltpu.get_barrier_semaphore()
    for i in (1, 2, 3):
        signal(barrier, at(y + i, xx, h))
        signal(barrier, at(y, xx + i, h))
        signal(barrier, at(y, xx, h + i))
    signal(barrier, at(y, xx, h, 1 - e))
    signal(barrier, at(y, xx, h, e, 1 - c))
    signal(barrier, at(y, xx, h, 1 - e, 1 - c))
    fetch.wait()
    pl.semaphore_wait(barrier, 12)
    for i in (1, 2, 3):
        signal(line_y, at(y + i, xx, h))

    def own_chip(i, start, size):
        part = own.at[grp, pl.ds(start, size)]
        return remote(part, part, own_send.at[1 + i], own_recv.at[1 + i], at(y, xx, h, 1 - e))

    own_chip(0, 0, EARLY).start()
    for i in (1, 2, 3):
        spread(0, 0, i)
        spread(i, 0, 0)
        spread(0, i, 0)
    pl.semaphore_wait(line_y, 3)
    for i in (1, 2, 3):
        signal(line_z, at(y, xx, h + i))
    lax.fori_loop(0, 9, spread_plane, 0)
    pl.semaphore_wait(line_z, 3)
    signal(other, at(y, xx, h, 1 - e))
    lax.fori_loop(0, 45, spread_rest, 0)
    own_core = remote(x, x, own_send.at[0], own_recv.at[0], at(y, xx, h, e, 1 - c))
    own_core.start()
    my_row = pl.multiple_of((h * 8 + y * 2 + xx // 2) * 16, 16)
    my_col = pl.multiple_of((xx % 2) * 512, 512)
    pieces[blk] = x[pl.ds(my_row, 16), pl.ds(my_col, 512)]

    def mate(g):
        return g + 4 - 8 * ((g // 4) % 2)

    def begin(g, carry):
        hop_a[0, g] = partners[1, partners[0, g]]
        hop_b[0, g] = mate(partners[2, g])
        low_a[g] = g
        low_b[g] = g
        return carry

    fetch_table.wait()
    lax.fori_loop(0, GROUPS, begin, 0)
    for step in range(5):
        now, later = step % 2, (step + 1) % 2

        def double(g, carry):
            s, t = hop_a[now, g], hop_b[now, g]
            low_a[g] = jnp.minimum(low_a[g], low_a[s])
            low_b[g] = jnp.minimum(low_b[g], low_b[t])
            hop_a[later, g] = hop_a[now, s]
            hop_b[later, g] = hop_b[now, t]
            return carry

        lax.fori_loop(0, GROUPS, double, 0)

    def first(g):
        return low_a[g] < low_a[partners[0, g]]

    def receives(g):
        return low_b[g] < low_b[partners[2, g]]

    def choose(g, carry):
        pick1[g] = jnp.where(first(g), partners[0, g], partners[1, g])
        back[g] = jnp.where(first(g), partners[1, g], partners[0, g])
        pick2[g] = partners[2, jnp.where(receives(g), g, mate(g))]
        return carry

    lax.fori_loop(0, GROUPS, choose, 0)

    own_acc[...] = jnp.zeros_like(own_acc)
    diagonal = lax.broadcasted_iota(jnp.int32, (ROWS, TILE), 0)
    across = lax.broadcasted_iota(jnp.int32, (ROWS, TILE), 1)

    for t in range(ROWS // TILE):
        terms = similarity(x[...], x[t * TILE : (t + 1) * TILE, :])
        terms = jnp.where(diagonal == across + t * TILE, 0.0, terms)
        own_acc[...] += terms[:, :128] + terms[:, 128:]

    def own_others(member):
        for t in range(ROWS // TILE):
            terms = similarity(x[...], own[member, t * TILE : (t + 1) * TILE, :])
            own_acc[...] += terms[:, :128] + terms[:, 128:]

    own_core.wait()
    own_others(e * 2 + 1 - c)

    drain(pieces.at[pl.ds(0, GROUPS - 1)], spread_recv)
    pl.semaphore_wait(other, 1)

    def place(k):
        d = k % 4
        ty, tx, th = (y + k // 16) % 4, (xx + (k // 4) % 4) % 4, (h + k) % 4
        to = jnp.where(d == 0, e, jnp.where(d == 1, 0, jnp.where(d == 3, 1, 1 - e)))
        second0 = jnp.where(e == 0, d, d - 1)
        second1 = jnp.where(e == 0, 3 - d, jnp.where(d == 0, 0, 1))
        slot = 2 * e + jnp.where(to == 0, second0, second1)
        row = pl.multiple_of(slot * 128 + (y * 2 + xx // 2) * 16, 16)
        return ty, tx, th, to, row

    def half_units(k, carry):
        ty, tx, th, to, row = place(k)
        lane = pl.multiple_of((tx % 2) * 256, 256)
        stage2[k] = pieces[pick2[ty * 16 + tx * 4 + th], :, pl.ds(lane, 256)]
        col = pl.multiple_of((xx % 2) * 512 + (tx % 2) * 256, 256)
        remote(
            stage2.at[k], met2.at[pl.ds(row, 16), pl.ds(col, 256)], send2, recv2, at(ty, tx, th, to)
        ).start()
        return carry

    def units(k, carry):
        ty, tx, th, to, row = place(k)
        stage1[k] = pieces[pick1[ty * 16 + tx * 4 + th]]
        remote(
            stage1.at[k], met1.at[pl.ds(row, 16), pl.ds(my_col, 512)], send1, recv1, at(ty, tx, th, to)
        ).start()
        return carry

    def paced(send, count, first_row):
        def group(i, carry):
            own_chip(1, pl.multiple_of(first_row + i * CHUNK, CHUNK), CHUNK).start()
            per = (GROUPS - 1) // count
            return lax.fori_loop(1 + i * per, 1 + (i + 1) * per, send, carry)

        lax.fori_loop(0, count, group, 0)

    paced(half_units, FEW, EARLY)
    paced(units, MANY, EARLY + FEW * CHUNK)
    home = pl.multiple_of((2 * e + 0) * 128 + (y * 2 + xx // 2) * 16, 16)
    half = pl.multiple_of((xx % 2) * 256, 256)
    met1[pl.ds(home, 16), pl.ds(my_col, 512)] = pieces[pick1[blk]]
    met2[pl.ds(home, 16), pl.ds(pl.multiple_of(my_col + half, 256), 256)] = pieces[
        pick2[blk], :, pl.ds(half, 256)
    ]

    def meet(met, acc, counts):
        acc[...] = jnp.zeros_like(acc)

        for t in range(4 * ROWS // TILE):
            member, part = t // 2, slice((t % 2) * TILE, (t % 2 + 1) * TILE)
            terms = similarity(met[...], own[member, part, :])
            acc[...] += terms[:, :128] + terms[:, 128:]
            sums = jnp.sum(terms.reshape(ROWS // 8, 8, TILE), axis=0)
            if counts is not None:
                row_acc[member, :, part] = jnp.where(counts, sums, 0.0)
            else:
                row_acc[member, :, part] += sums

    drain(stage2.at[pl.ds(0, GROUPS - 1)], recv2)
    pair = at(y, xx + 1 - 2 * (xx % 2), h)
    for i in range(2):
        columns = pl.ds(pl.multiple_of(i * 512 + half, 256), 256)
        remote(met2.at[:, columns], met2.at[:, columns], fwd_send.at[i], fwd_recv.at[i], pair).start()
    own_chip(0, 0, EARLY).wait()
    own_chip(1, EARLY, ROWS - EARLY).wait()
    across_core = remote(
        own.at[2 - 2 * e + c], own.at[2 - 2 * e + c], own_send.at[3], own_recv.at[3], at(y, xx, h, e, 1 - c)
    )
    across_core.start()
    own_others(2 - 2 * e + c)
    across_core.wait()
    own_others(2 - 2 * e + 1 - c)
    for i in range(2):
        columns = pl.ds(pl.multiple_of(i * 512 + half, 256), 256)
        remote(met2.at[:, columns], met2.at[:, columns], fwd_send.at[i], fwd_recv.at[i], pair).wait()
    meet(met2, acc2, receives(blk))

    def publish(u, acc):
        sums = lane_sums(acc[...])
        for s in range(4):
            col_out[s // 2, u, pl.ds(s % 2, 1), :] = sums[0:1, s * 128 : (s + 1) * 128]

    publish(1, acc2)
    own_sums = lane_sums(own_acc[...])[0:1, :]

    drain(stage1.at[pl.ds(0, GROUPS - 1)], recv1)
    meet(met1, acc1, None)

    publish(0, acc1)
    for i in range(1, 8):
        th, te = (h + i // 2) % 4, (e + i) % 2
        remote(
            col_out.at[te], col_line.at[2 * h + e], col_send.at[0], col_recv.at[0], at(y, xx, th, te)
        ).start()
    col_line[2 * h + e] = col_out[e]
    siblings = []
    for i in (1, 2, 3):
        member = (grp + i) % 4
        copy = remote(
            row_acc.at[member], row_in.at[i - 1], row_send.at[i - 1], row_recv.at[i - 1], (blk, member)
        )
        copy.start()
        siblings.append(copy)
    drain(col_line.at[pl.ds(0, 7)], col_recv.at[0])

    def give(k):
        ty, tx = (y + k // 4) % 4, (xx + k % 4) % 4
        other_blk = ty * 16 + tx * 4 + h
        for u, a in ((0, back[other_blk]), (1, partners[2, other_blk])):
            for i in range(2):
                col_stage[k, u, i] = col_line[2 * (a % 4) + i, u]
        return ty, tx

    def give_peer(k, carry):
        ty, tx = give(k)
        remote(
            col_stage.at[k], col_plane.at[y * 4 + xx], col_send.at[1], col_recv.at[1], at(ty, tx, h)
        ).start()
        return carry

    lax.fori_loop(1, 16, give_peer, 0)
    give(0)
    col_plane[y * 4 + xx] = col_stage[0]
    for copy in siblings:
        copy.wait()
    total = row_acc[grp] + row_in[0] + row_in[1] + row_in[2]
    density = jnp.sum(total, axis=0, keepdims=True) + own_sums
    drain(col_plane.at[pl.ds(0, 15)], col_recv.at[1])
    silent = jnp.logical_not(receives(blk))

    def column_sums(a, u, q):
        d = (a % 4 - q + 4) % 4
        j0 = jnp.where(d == 2, 3, jnp.where(d == 3, 2, d))
        j1 = jnp.where(d == 0, 2, jnp.where(d == 3, 3, d - 1))
        j = jnp.where(e == 0, j0, j1)
        return col_plane[a // 4, u, j // 2, pl.ds(j % 2, 1), :]

    for q in range(4):
        part = density[:, q * 128 : (q + 1) * 128] + column_sums(back[blk], 0, q)
        part = part + jnp.where(silent, column_sums(partners[2, blk], 1, q), 0.0)
        out[pl.ds(q, 1), :] = part

    drain(pieces.at[pl.ds(0, GROUPS - 1)], spread_send)
    drain(stage1.at[pl.ds(0, GROUPS - 1)], send1)
    drain(stage2.at[pl.ds(0, GROUPS - 1)], send2)
    drain(col_line.at[pl.ds(0, 7)], col_send.at[0])
    drain(col_plane.at[pl.ds(0, 15)], col_send.at[1])


def body(embeddings, partners):
    f32, bf16, dma = jnp.float32, jnp.bfloat16, pltpu.SemaphoreType.DMA
    regular = pltpu.SemaphoreType.REGULAR
    density = pl.pallas_call(
        kernel,
        out_shape=jax.ShapeDtypeStruct((4, 128), f32),
        in_specs=[
            pl.BlockSpec(memory_space=pl.ANY),
            pl.BlockSpec(memory_space=pl.ANY),
        ],
        out_specs=pl.BlockSpec(memory_space=pltpu.VMEM),
        scratch_shapes=[
            pltpu.VMEM((4, ROWS, WIDTH), bf16),
            pltpu.VMEM((GROUPS, 16, 512), bf16),
            pltpu.VMEM((GROUPS, 16, 512), bf16),
            pltpu.VMEM((GROUPS, 16, 256), bf16),
            pltpu.VMEM((ROWS, WIDTH), bf16),
            pltpu.VMEM((ROWS, WIDTH), bf16),
            pltpu.VMEM((ROWS, 128), f32),
            pltpu.VMEM((ROWS, 128), f32),
            pltpu.VMEM((ROWS, 128), f32),
            pltpu.VMEM((4, 8, ROWS), f32),
            pltpu.VMEM((3, 8, ROWS), f32),
            pltpu.VMEM((2, 2, 2, 128), f32),
            pltpu.VMEM((8, 2, 2, 128), f32),
            pltpu.VMEM((16, 2, 2, 2, 128), f32),
            pltpu.VMEM((16, 2, 2, 2, 128), f32),
            pltpu.SMEM((3, GROUPS), jnp.int32),
            pltpu.SMEM((2, GROUPS), jnp.int32),
            pltpu.SMEM((GROUPS,), jnp.int32),
            pltpu.SMEM((2, GROUPS), jnp.int32),
            pltpu.SMEM((GROUPS,), jnp.int32),
            pltpu.SMEM((GROUPS,), jnp.int32),
            pltpu.SMEM((GROUPS,), jnp.int32),
            pltpu.SMEM((GROUPS,), jnp.int32),
            regular, regular, regular,
            dma, dma, dma, dma, dma, dma,
            dma, dma, dma((4,)), dma((4,)), dma((2,)), dma((2,)), dma((3,)), dma((3,)), dma((2,)), dma((2,)),
        ],
        compiler_params=pltpu.CompilerParams(
            collective_id=0, has_side_effects=True, vmem_limit_bytes=60 * 2**20
        ),
        cost_estimate=pl.CostEstimate(
            flops=2 * 4 * ROWS * 3 * ROWS * WIDTH, bytes_accessed=2**20, transcendentals=12 * ROWS * ROWS
        ),
    )(partners, embeddings)
    return density.reshape(ROWS)


def solution(mesh):
    return jax.shard_map(
        body,
        mesh=mesh,
        in_specs=(P(("blk", "grp"), None), P()),
        out_specs=P(("blk", "grp")),
        check_vma=False,
    )
```

```python
import math

import jax
import jax.numpy as jnp
from jax import lax
from jax.experimental import pallas as pl
from jax.experimental.pallas import tpu as pltpu
from jax.sharding import PartitionSpec as P

MESH = pl.DeviceIdType.MESH
HEAT = 0.05
RATE = math.log2(math.e) / HEAT
GROUPS = 64
ROWS = 512
WIDTH = 1024
TILE = 256
EARLY = 64
FEW, FEW_ROWS = 7, 16
MANY, MANY_ROWS = 21, 16


def similarity(columns, members):
    c = lax.dot_general(columns, members, (((1,), (1,)), ((), ())), preferred_element_type=jnp.float32)
    return jnp.exp2(c * RATE - RATE)


def lane_sums(total):
    ones = jnp.ones((8, 128), jnp.float32)
    return lax.dot_general(
        ones, total, (((1,), (1,)), ((), ())),
        precision=lax.Precision.HIGHEST, preferred_element_type=jnp.float32,
    )


def kernel(
    rounds, rows, out,
    own, pieces, stage1, stage2, met1, met2, own_acc, acc1, acc2, row_acc, row_in, col_out, col_line, col_stage, col_plane,
    partners, hop_a, low_a, hop_b, low_b, pick1, pick2, back,
    line_y, line_h, line_z, other, spread_send, spread_recv, send1, recv1, send2, recv2,
    load, table, own_send, own_recv, fwd_send, fwd_recv, row_send, row_recv, col_send, col_recv,
):
    blk, grp = lax.axis_index("blk"), lax.axis_index("grp")
    y, xx, h = blk // 16, (blk // 4) % 4, blk % 4
    e, c = grp // 2, grp % 2

    def at(y_, x_, h_, e_=None, c_=None):
        e_ = e if e_ is None else e_
        c_ = c if c_ is None else c_
        return ((y_ % 4) * 16 + (x_ % 4) * 4 + h_ % 4, e_ * 2 + c_)

    def signal(sem, device):
        pl.semaphore_signal(sem, inc=1, device_id=device, device_id_type=MESH)

    def remote(src, dst, send, recv, device):
        return pltpu.make_async_remote_copy(
            src_ref=src, dst_ref=dst, send_sem=send, recv_sem=recv, device_id=device, device_id_type=MESH
        )

    def drain(ref, sem):
        pltpu.make_async_copy(ref, ref, sem).wait()

    x = own.at[grp]
    fetch = pltpu.make_async_copy(rows, x, load)
    fetch.start()
    fetch_table = pltpu.make_async_copy(rounds, partners, table)
    fetch_table.start()

    def spread(dy, dx, dh):
        ty, tx, th = (y + dy) % 4, (xx + dx) % 4, (h + dh) % 4
        row = pl.multiple_of((th * 8 + ty * 2 + tx // 2) * 16, 16)
        col = pl.multiple_of((tx % 2) * 512, 512)
        remote(
            x.at[pl.ds(row, 16), pl.ds(col, 512)], pieces.at[blk], spread_send, spread_recv, at(ty, tx, th)
        ).start()

    def spread_lines(j, carry):
        spread(1 + j // 3, 0, 1 + j % 3)
        spread(0, 1 + j // 3, 1 + j % 3)
        return carry

    def spread_plane(j, carry):
        spread(1 + j // 3, 1 + j % 3, 0)
        return carry

    def spread_rest(j, carry):
        spread(1 + j // 9, 1 + (j // 3) % 3, 1 + j % 3)
        return carry

    barrier = pltpu.get_barrier_semaphore()
    for i in (1, 2, 3):
        signal(barrier, at(y + i, xx, h))
        signal(barrier, at(y, xx + i, h))
        signal(barrier, at(y, xx, h + i))
    signal(barrier, at(y, xx, h, 1 - e))
    signal(barrier, at(y, xx, h, e, 1 - c))
    signal(barrier, at(y, xx, h, 1 - e, 1 - c))
    fetch.wait()
    pl.semaphore_wait(barrier, 12)
    for i in (1, 2, 3):
        signal(line_y, at(y + i, xx, h))
        signal(line_h, at(y, xx, h + i))

    def own_chip(i, start, size):
        part = own.at[grp, pl.ds(start, size)]
        return remote(part, part, own_send.at[1 + i], own_recv.at[1 + i], at(y, xx, h, 1 - e))

    own_chip(0, 0, EARLY).start()
    for i in (1, 2, 3):
        spread(0, 0, i)
        spread(i, 0, 0)
        spread(0, i, 0)
    pl.semaphore_wait(line_y, 3)
    for i in (1, 2, 3):
        signal(line_z, at(y, xx, h + i))
    pl.semaphore_wait(line_h, 3)
    lax.fori_loop(0, 9, spread_lines, 0)
    pl.semaphore_wait(line_z, 3)
    signal(other, at(y, xx, h, 1 - e))
    lax.fori_loop(0, 27, spread_rest, 0)
    lax.fori_loop(0, 9, spread_plane, 0)
    own_core = remote(x, x, own_send.at[0], own_recv.at[0], at(y, xx, h, e, 1 - c))
    own_core.start()
    my_row = pl.multiple_of((h * 8 + y * 2 + xx // 2) * 16, 16)
    my_col = pl.multiple_of((xx % 2) * 512, 512)
    pieces[blk] = x[pl.ds(my_row, 16), pl.ds(my_col, 512)]

    def mate(g):
        return g + 4 - 8 * ((g // 4) % 2)

    def begin(g, carry):
        hop_a[0, g] = partners[1, partners[0, g]]
        hop_b[0, g] = mate(partners[2, g])
        low_a[g] = g
        low_b[g] = g
        return carry

    fetch_table.wait()
    lax.fori_loop(0, GROUPS, begin, 0)
    for step in range(5):
        now, later = step % 2, (step + 1) % 2

        def double(g, carry):
            s, t = hop_a[now, g], hop_b[now, g]
            low_a[g] = jnp.minimum(low_a[g], low_a[s])
            low_b[g] = jnp.minimum(low_b[g], low_b[t])
            hop_a[later, g] = hop_a[now, s]
            hop_b[later, g] = hop_b[now, t]
            return carry

        lax.fori_loop(0, GROUPS, double, 0)

    def first(g):
        return low_a[g] < low_a[partners[0, g]]

    def receives(g):
        return low_b[g] < low_b[partners[2, g]]

    def choose(g, carry):
        pick1[g] = jnp.where(first(g), partners[0, g], partners[1, g])
        back[g] = jnp.where(first(g), partners[1, g], partners[0, g])
        pick2[g] = partners[2, jnp.where(receives(g), g, mate(g))]
        return carry

    lax.fori_loop(0, GROUPS, choose, 0)

    own_acc[...] = jnp.zeros_like(own_acc)
    diagonal = lax.broadcasted_iota(jnp.int32, (ROWS, TILE), 0)
    across = lax.broadcasted_iota(jnp.int32, (ROWS, TILE), 1)

    for t in range(ROWS // TILE):
        terms = similarity(x[...], x[t * TILE : (t + 1) * TILE, :])
        terms = jnp.where(diagonal == across + t * TILE, 0.0, terms)
        own_acc[...] += terms[:, :128] + terms[:, 128:]

    def own_others(member):
        for t in range(ROWS // TILE):
            terms = similarity(x[...], own[member, t * TILE : (t + 1) * TILE, :])
            own_acc[...] += terms[:, :128] + terms[:, 128:]

    own_core.wait()
    own_others(e * 2 + 1 - c)

    drain(pieces.at[pl.ds(0, GROUPS - 1)], spread_recv)
    pl.semaphore_wait(other, 1)

    def place(k):
        d = k % 4
        ty, tx, th = (y + k // 16) % 4, (xx + (k // 4) % 4) % 4, (h + k) % 4
        to = jnp.where(d == 0, e, jnp.where(d == 1, 0, jnp.where(d == 3, 1, 1 - e)))
        second0 = jnp.where(e == 0, d, d - 1)
        second1 = jnp.where(e == 0, 3 - d, jnp.where(d == 0, 0, 1))
        slot = 2 * e + jnp.where(to == 0, second0, second1)
        row = pl.multiple_of(slot * 128 + (y * 2 + xx // 2) * 16, 16)
        return ty, tx, th, to, row

    def half_units(k, carry):
        ty, tx, th, to, row = place(k)
        lane = pl.multiple_of((tx % 2) * 256, 256)
        stage2[k] = pieces[pick2[ty * 16 + tx * 4 + th], :, pl.ds(lane, 256)]
        col = pl.multiple_of((xx % 2) * 512 + (tx % 2) * 256, 256)
        remote(
            stage2.at[k], met2.at[pl.ds(row, 16), pl.ds(col, 256)], send2, recv2, at(ty, tx, th, to)
        ).start()
        return carry

    def units(k, carry):
        ty, tx, th, to, row = place(k)
        stage1[k] = pieces[pick1[ty * 16 + tx * 4 + th]]
        remote(
            stage1.at[k], met1.at[pl.ds(row, 16), pl.ds(my_col, 512)], send1, recv1, at(ty, tx, th, to)
        ).start()
        return carry

    def paced(send, count, per, first_row, rows_each):
        def group(i, carry):
            start = pl.multiple_of(first_row + i * rows_each, 16)
            own_chip(1, start, rows_each).start()
            return lax.fori_loop(1 + i * per, 1 + (i + 1) * per, send, carry)

        lax.fori_loop(0, count, group, 0)

    paced(half_units, FEW, (GROUPS - 1) // FEW, EARLY, FEW_ROWS)
    paced(units, MANY, 3, EARLY + FEW * FEW_ROWS, MANY_ROWS)
    lax.fori_loop(1 + 3 * MANY, GROUPS, units, 0)
    home = pl.multiple_of((2 * e + 0) * 128 + (y * 2 + xx // 2) * 16, 16)
    half = pl.multiple_of((xx % 2) * 256, 256)
    met1[pl.ds(home, 16), pl.ds(my_col, 512)] = pieces[pick1[blk]]
    met2[pl.ds(home, 16), pl.ds(pl.multiple_of(my_col + half, 256), 256)] = pieces[
        pick2[blk], :, pl.ds(half, 256)
    ]

    def meet(met, acc, counts, member):
        for t in range(ROWS // TILE):
            part = slice(t * TILE, (t + 1) * TILE)
            terms = similarity(met[...], own[member, part, :])
            acc[...] += terms[:, :128] + terms[:, 128:]
            sums = jnp.sum(terms.reshape(ROWS // 8, 8, TILE), axis=0)
            if counts is not None:
                row_acc[member, :, part] = jnp.where(counts, sums, 0.0)
            else:
                row_acc[member, :, part] += sums

    drain(stage2.at[pl.ds(0, GROUPS - 1)], recv2)
    pair = at(y, xx + 1 - 2 * (xx % 2), h)
    for i in range(2):
        columns = pl.ds(pl.multiple_of(i * 512 + half, 256), 256)
        remote(met2.at[:, columns], met2.at[:, columns], fwd_send.at[i], fwd_recv.at[i], pair).start()
    acc1[...] = jnp.zeros_like(acc1)
    acc2[...] = jnp.zeros_like(acc2)
    for i in range(2):
        columns = pl.ds(pl.multiple_of(i * 512 + half, 256), 256)
        remote(met2.at[:, columns], met2.at[:, columns], fwd_send.at[i], fwd_recv.at[i], pair).wait()
    counts = receives(blk)
    meet(met2, acc2, counts, grp)
    meet(met2, acc2, counts, 2 * e + 1 - c)
    own_chip(0, 0, EARLY).wait()
    own_chip(1, EARLY, ROWS - EARLY).wait()
    across_core = remote(
        own.at[2 - 2 * e + c], own.at[2 - 2 * e + c], own_send.at[3], own_recv.at[3], at(y, xx, h, e, 1 - c)
    )
    across_core.start()
    own_others(2 - 2 * e + c)
    meet(met2, acc2, counts, 2 - 2 * e + c)
    across_core.wait()
    own_others(2 - 2 * e + 1 - c)
    meet(met2, acc2, counts, 2 - 2 * e + 1 - c)

    def publish(u, acc):
        sums = lane_sums(acc[...])
        for s in range(4):
            col_out[s // 2, u, pl.ds(s % 2, 1), :] = sums[0:1, s * 128 : (s + 1) * 128]

    publish(1, acc2)
    own_sums = lane_sums(own_acc[...])[0:1, :]

    drain(stage1.at[pl.ds(0, GROUPS - 1)], recv1)
    for member in range(4):
        meet(met1, acc1, None, member)

    publish(0, acc1)
    for i in range(1, 8):
        th, te = (h + i // 2) % 4, (e + i) % 2
        remote(
            col_out.at[te], col_line.at[2 * h + e], col_send.at[0], col_recv.at[0], at(y, xx, th, te)
        ).start()
    col_line[2 * h + e] = col_out[e]
    siblings = []
    for i in (1, 2, 3):
        member = (grp + i) % 4
        copy = remote(
            row_acc.at[member], row_in.at[i - 1], row_send.at[i - 1], row_recv.at[i - 1], (blk, member)
        )
        copy.start()
        siblings.append(copy)
    drain(col_line.at[pl.ds(0, 7)], col_recv.at[0])

    def give(k):
        ty, tx = (y + k // 4) % 4, (xx + k % 4) % 4
        other_blk = ty * 16 + tx * 4 + h
        for u, a in ((0, back[other_blk]), (1, partners[2, other_blk])):
            for i in range(2):
                col_stage[k, u, i] = col_line[2 * (a % 4) + i, u]
        return ty, tx

    def give_peer(k):
        ty, tx = give(k)
        remote(
            col_stage.at[k], col_plane.at[y * 4 + xx], col_send.at[1], col_recv.at[1], at(ty, tx, h)
        ).start()

    for k in range(1, 16):
        give_peer(k)
    give(0)
    col_plane[y * 4 + xx] = col_stage[0]
    for copy in siblings:
        copy.wait()
    total = row_acc[grp] + row_in[0] + row_in[1] + row_in[2]
    density = jnp.sum(total, axis=0, keepdims=True) + own_sums
    drain(col_plane.at[pl.ds(0, 15)], col_recv.at[1])
    silent = jnp.logical_not(receives(blk))

    def column_sums(a, u, q):
        d = (a % 4 - q + 4) % 4
        j0 = jnp.where(d == 2, 3, jnp.where(d == 3, 2, d))
        j1 = jnp.where(d == 0, 2, jnp.where(d == 3, 3, d - 1))
        j = jnp.where(e == 0, j0, j1)
        return col_plane[a // 4, u, j // 2, pl.ds(j % 2, 1), :]

    for q in range(4):
        part = density[:, q * 128 : (q + 1) * 128] + column_sums(back[blk], 0, q)
        part = part + jnp.where(silent, column_sums(partners[2, blk], 1, q), 0.0)
        out[pl.ds(q, 1), :] = part

    drain(pieces.at[pl.ds(0, GROUPS - 1)], spread_send)
    drain(stage1.at[pl.ds(0, GROUPS - 1)], send1)
    drain(stage2.at[pl.ds(0, GROUPS - 1)], send2)
    drain(col_line.at[pl.ds(0, 7)], col_send.at[0])
    drain(col_plane.at[pl.ds(0, 15)], col_send.at[1])


def body(embeddings, partners):
    f32, bf16, dma = jnp.float32, jnp.bfloat16, pltpu.SemaphoreType.DMA
    regular = pltpu.SemaphoreType.REGULAR
    density = pl.pallas_call(
        kernel,
        out_shape=jax.ShapeDtypeStruct((4, 128), f32),
        in_specs=[
            pl.BlockSpec(memory_space=pl.ANY),
            pl.BlockSpec(memory_space=pl.ANY),
        ],
        out_specs=pl.BlockSpec(memory_space=pltpu.VMEM),
        scratch_shapes=[
            pltpu.VMEM((4, ROWS, WIDTH), bf16),
            pltpu.VMEM((GROUPS, 16, 512), bf16),
            pltpu.VMEM((GROUPS, 16, 512), bf16),
            pltpu.VMEM((GROUPS, 16, 256), bf16),
            pltpu.VMEM((ROWS, WIDTH), bf16),
            pltpu.VMEM((ROWS, WIDTH), bf16),
            pltpu.VMEM((ROWS, 128), f32),
            pltpu.VMEM((ROWS, 128), f32),
            pltpu.VMEM((ROWS, 128), f32),
            pltpu.VMEM((4, 8, ROWS), f32),
            pltpu.VMEM((3, 8, ROWS), f32),
            pltpu.VMEM((2, 2, 2, 128), f32),
            pltpu.VMEM((8, 2, 2, 128), f32),
            pltpu.VMEM((16, 2, 2, 2, 128), f32),
            pltpu.VMEM((16, 2, 2, 2, 128), f32),
            pltpu.SMEM((3, GROUPS), jnp.int32),
            pltpu.SMEM((2, GROUPS), jnp.int32),
            pltpu.SMEM((GROUPS,), jnp.int32),
            pltpu.SMEM((2, GROUPS), jnp.int32),
            pltpu.SMEM((GROUPS,), jnp.int32),
            pltpu.SMEM((GROUPS,), jnp.int32),
            pltpu.SMEM((GROUPS,), jnp.int32),
            pltpu.SMEM((GROUPS,), jnp.int32),
            regular, regular, regular, regular,
            dma, dma, dma, dma, dma, dma,
            dma, dma, dma((4,)), dma((4,)), dma((2,)), dma((2,)), dma((3,)), dma((3,)), dma((2,)), dma((2,)),
        ],
        compiler_params=pltpu.CompilerParams(
            collective_id=0, has_side_effects=True, vmem_limit_bytes=60 * 2**20
        ),
        cost_estimate=pl.CostEstimate(
            flops=2 * 4 * ROWS * 3 * ROWS * WIDTH, bytes_accessed=2**20, transcendentals=12 * ROWS * ROWS
        ),
    )(partners, embeddings)
    return density.reshape(ROWS)


def solution(mesh):
    return jax.shard_map(
        body,
        mesh=mesh,
        in_specs=(P(("blk", "grp"), None), P()),
        out_specs=P(("blk", "grp")),
        check_vma=False,
    )
```

```python
import math

import jax
import jax.numpy as jnp
from jax import lax
from jax.experimental import pallas as pl
from jax.experimental.pallas import tpu as pltpu
from jax.sharding import PartitionSpec as P

MESH = pl.DeviceIdType.MESH
HEAT = 0.05
RATE = math.log2(math.e) / HEAT
GROUPS = 64
ROWS = 512
WIDTH = 1024
TILE = 256
EARLY = 64
PACE = ((7, 16), (21, 16))


def similarity(columns, members):
    c = lax.dot_general(columns, members, (((1,), (1,)), ((), ())), preferred_element_type=jnp.float32)
    return jnp.exp2(c * RATE - RATE)


def lane_sums(total):
    parts = [jnp.sum(total[s * 128 : (s + 1) * 128].T, axis=0, keepdims=True) for s in range(4)]
    return jnp.concatenate(parts, axis=1)


def kernel(
    rounds, rows, out,
    own, pieces_a, pieces_b, stage1, stage2, met1, met2, own_acc, acc1, acc2, row_acc, row_in, col_out, col_line, col_stage, col_plane,
    partners, hop_a, low_a, hop_b, low_b, pick1, pick2, back,
    line_y, line_h, line_z, other, spread_send, spread_recv, send1, recv1, send2, recv2,
    load, table, own_send, own_recv, fwd_send, fwd_recv, row_send, row_recv, col_send, col_recv,
):
    blk, grp = lax.axis_index("blk"), lax.axis_index("grp")
    pieces = (pieces_a, pieces_b)
    y, xx, h = blk // 16, (blk // 4) % 4, blk % 4
    e, c = grp // 2, grp % 2

    def at(y_, x_, h_, e_=None, c_=None):
        e_ = e if e_ is None else e_
        c_ = c if c_ is None else c_
        return ((y_ % 4) * 16 + (x_ % 4) * 4 + h_ % 4, e_ * 2 + c_)

    def signal(sem, device):
        pl.semaphore_signal(sem, inc=1, device_id=device, device_id_type=MESH)

    def remote(src, dst, send, recv, device):
        return pltpu.make_async_remote_copy(
            src_ref=src, dst_ref=dst, send_sem=send, recv_sem=recv, device_id=device, device_id_type=MESH
        )

    def drain(ref, sem):
        pltpu.make_async_copy(ref, ref, sem).wait()

    x = own.at[grp]
    fetch = pltpu.make_async_copy(rows, x, load)
    fetch.start()
    fetch_table = pltpu.make_async_copy(rounds, partners, table)
    fetch_table.start()

    def spread(dy, dx, dh, part=0):
        ty, tx, th = (y + dy) % 4, (xx + dx) % 4, (h + dh) % 4
        row = pl.multiple_of((th * 8 + ty * 2 + tx // 2) * 16, 16)
        col = pl.multiple_of((tx % 2) * 512 + part * 256, 256)
        remote(
            x.at[pl.ds(row, 16), pl.ds(col, 256)],
            pieces[part].at[blk],
            spread_send.at[part],
            spread_recv.at[part],
            at(ty, tx, th),
        ).start()

    def spread_lines(j, carry):
        spread(1 + j // 3, 0, 1 + j % 3)
        spread(0, 1 + j // 3, 1 + j % 3)
        return carry

    def spread_plane(j, carry):
        spread(1 + j // 3, 1 + j % 3, 0)
        return carry

    def spread_rest(j, carry):
        spread(1 + j // 9, 1 + (j // 3) % 3, 1 + j % 3)
        return carry

    barrier = pltpu.get_barrier_semaphore()
    for i in (1, 2, 3):
        signal(barrier, at(y + i, xx, h))
        signal(barrier, at(y, xx + i, h))
        signal(barrier, at(y, xx, h + i))
    signal(barrier, at(y, xx, h, 1 - e))
    signal(barrier, at(y, xx, h, e, 1 - c))
    signal(barrier, at(y, xx, h, 1 - e, 1 - c))
    fetch.wait()
    pl.semaphore_wait(barrier, 12)
    for i in (1, 2, 3):
        signal(line_y, at(y + i, xx, h))
        signal(line_h, at(y, xx, h + i))

    def own_chip(i, start, size):
        part = own.at[grp, pl.ds(start, size)]
        return remote(part, part, own_send.at[1 + i], own_recv.at[1 + i], at(y, xx, h, 1 - e))

    own_chip(0, 0, EARLY).start()
    for i in (1, 2, 3):
        spread(0, 0, i)
        spread(i, 0, 0)
        spread(0, i, 0)
    pl.semaphore_wait(line_y, 3)
    for i in (1, 2, 3):
        signal(line_z, at(y, xx, h + i))
    pl.semaphore_wait(line_h, 3)
    lax.fori_loop(0, 9, spread_lines, 0)
    pl.semaphore_wait(line_z, 3)
    signal(other, at(y, xx, h, 1 - e))
    lax.fori_loop(0, 27, spread_rest, 0)
    lax.fori_loop(0, 9, spread_plane, 0)

    def spread_second(k, carry):
        spread(k // 16, (k // 4) % 4, k % 4, 1)
        return carry

    lax.fori_loop(1, GROUPS, spread_second, 0)
    own_core = remote(x, x, own_send.at[0], own_recv.at[0], at(y, xx, h, e, 1 - c))
    own_core.start()
    my_row = pl.multiple_of((h * 8 + y * 2 + xx // 2) * 16, 16)
    my_col = pl.multiple_of((xx % 2) * 512, 512)
    for part in range(2):
        lanes = pl.ds(pl.multiple_of(my_col + part * 256, 256), 256)
        pieces[part][blk] = x[pl.ds(my_row, 16), lanes]

    def mate(g):
        return g + 4 - 8 * ((g // 4) % 2)

    def begin(g, carry):
        hop_a[0, g] = partners[1, partners[0, g]]
        hop_b[0, g] = mate(partners[2, g])
        low_a[g] = g
        low_b[g] = g
        return carry

    fetch_table.wait()
    lax.fori_loop(0, GROUPS, begin, 0)
    for step in range(5):
        now, later = step % 2, (step + 1) % 2

        def double(g, carry):
            s, t = hop_a[now, g], hop_b[now, g]
            low_a[g] = jnp.minimum(low_a[g], low_a[s])
            low_b[g] = jnp.minimum(low_b[g], low_b[t])
            hop_a[later, g] = hop_a[now, s]
            hop_b[later, g] = hop_b[now, t]
            return carry

        lax.fori_loop(0, GROUPS, double, 0)

    def first(g):
        return low_a[g] < low_a[partners[0, g]]

    def receives(g):
        return low_b[g] < low_b[partners[2, g]]

    def choose(g, carry):
        pick1[g] = jnp.where(first(g), partners[0, g], partners[1, g])
        back[g] = jnp.where(first(g), partners[1, g], partners[0, g])
        pick2[g] = partners[2, jnp.where(receives(g), g, mate(g))]
        return carry

    lax.fori_loop(0, GROUPS, choose, 0)

    own_acc[...] = jnp.zeros_like(own_acc)
    diagonal = lax.broadcasted_iota(jnp.int32, (ROWS, TILE), 0)
    across = lax.broadcasted_iota(jnp.int32, (ROWS, TILE), 1)

    for t in range(ROWS // TILE):
        terms = similarity(x[...], x[t * TILE : (t + 1) * TILE, :])
        terms = jnp.where(diagonal == across + t * TILE, 0.0, terms)
        own_acc[...] += terms[:, :128] + terms[:, 128:]

    def own_others(member):
        for t in range(ROWS // TILE):
            terms = similarity(x[...], own[member, t * TILE : (t + 1) * TILE, :])
            own_acc[...] += terms[:, :128] + terms[:, 128:]

    own_core.wait()
    own_others(e * 2 + 1 - c)

    def place(k):
        d = k % 4
        ty, tx, th = (y + k // 16) % 4, (xx + (k // 4) % 4) % 4, (h + k) % 4
        to = jnp.where(d == 0, e, jnp.where(d == 1, 0, jnp.where(d == 3, 1, 1 - e)))
        second0 = jnp.where(e == 0, d, d - 1)
        second1 = jnp.where(e == 0, 3 - d, jnp.where(d == 0, 0, 1))
        slot = 2 * e + jnp.where(to == 0, second0, second1)
        row = pl.multiple_of(slot * 128 + (y * 2 + xx // 2) * 16, 16)
        return ty, tx, th, to, row

    half = pl.multiple_of((xx % 2) * 256, 256)
    home = pl.multiple_of((2 * e + 0) * 128 + (y * 2 + xx // 2) * 16, 16)

    def half_units(part):
        def send(j, carry):
            k = (j // 8) * 16 + (2 * ((j // 4) % 2) + (part + xx) % 2) * 4 + j % 4
            ty, tx, th, to, row = place(k)
            stage2[k] = pieces[part][pick2[ty * 16 + tx * 4 + th]]
            col = pl.multiple_of((xx % 2) * 512 + part * 256, 256)
            remote(
                stage2.at[k], met2.at[pl.ds(row, 16), pl.ds(col, 256)], send2, recv2, at(ty, tx, th, to)
            ).start()
            return carry

        lax.fori_loop(1 - (part + xx) % 2, GROUPS // 2, send, 0)

    def units(part, first_row):
        count, size = PACE[part]
        per = (GROUPS - 1) // count

        def send(k, carry):
            ty, tx, th, to, row = place(k)
            stage1[part, k] = pieces[part][pick1[ty * 16 + tx * 4 + th]]
            col = pl.multiple_of(my_col + part * 256, 256)
            remote(
                stage1.at[part, k],
                met1.at[pl.ds(row, 16), pl.ds(col, 256)],
                send1.at[part],
                recv1.at[part],
                at(ty, tx, th, to),
            ).start()
            return carry

        def group(i, carry):
            own_chip(1, pl.multiple_of(first_row + i * size, 16), size).start()
            return lax.fori_loop(1 + i * per, 1 + (i + 1) * per, send, carry)

        lax.fori_loop(0, count, group, 0)
        lax.fori_loop(1 + count * per, GROUPS, send, 0)
        met1[pl.ds(home, 16), pl.ds(pl.multiple_of(my_col + part * 256, 256), 256)] = pieces[part][pick1[blk]]

    drain(pieces_a.at[pl.ds(0, GROUPS - 1)], spread_recv.at[0])
    pl.semaphore_wait(other, 1)
    half_units(0)
    drain(pieces_b.at[pl.ds(0, GROUPS - 1)], spread_recv.at[1])
    half_units(1)
    units(0, EARLY)
    units(1, EARLY + PACE[0][0] * PACE[0][1])
    met2[pl.ds(home, 16), pl.ds(pl.multiple_of(my_col + half, 256), 256)] = jnp.where(
        xx % 2 == 0, pieces_a[pick2[blk]], pieces_b[pick2[blk]]
    )

    def meet(met, acc, counts, member):
        for t in range(ROWS // TILE):
            part = slice(t * TILE, (t + 1) * TILE)
            terms = similarity(met[...], own[member, part, :])
            acc[...] += terms[:, :128] + terms[:, 128:]
            sums = jnp.sum(terms.reshape(ROWS // 8, 8, TILE), axis=0)
            if counts is not None:
                row_acc[member, :, part] = jnp.where(counts, sums, 0.0)
            else:
                row_acc[member, :, part] += sums

    drain(stage2.at[pl.ds(0, GROUPS - 1)], recv2)
    pair = at(y, xx + 1 - 2 * (xx % 2), h)
    for i in range(2):
        columns = pl.ds(pl.multiple_of(i * 512 + half, 256), 256)
        remote(met2.at[:, columns], met2.at[:, columns], fwd_send.at[i], fwd_recv.at[i], pair).start()
    acc1[...] = jnp.zeros_like(acc1)
    acc2[...] = jnp.zeros_like(acc2)
    for i in range(2):
        columns = pl.ds(pl.multiple_of(i * 512 + half, 256), 256)
        remote(met2.at[:, columns], met2.at[:, columns], fwd_send.at[i], fwd_recv.at[i], pair).wait()
    counts = receives(blk)
    meet(met2, acc2, counts, grp)
    meet(met2, acc2, counts, 2 * e + 1 - c)
    own_chip(0, 0, EARLY).wait()
    own_chip(1, EARLY, ROWS - EARLY).wait()
    across_core = remote(
        own.at[2 - 2 * e + c], own.at[2 - 2 * e + c], own_send.at[3], own_recv.at[3], at(y, xx, h, e, 1 - c)
    )
    across_core.start()
    own_others(2 - 2 * e + c)
    meet(met2, acc2, counts, 2 - 2 * e + c)
    across_core.wait()
    own_others(2 - 2 * e + 1 - c)
    meet(met2, acc2, counts, 2 - 2 * e + 1 - c)

    def publish(u, acc):
        sums = lane_sums(acc[...])
        for s in range(4):
            col_out[s // 2, u, pl.ds(s % 2, 1), :] = sums[:, s * 128 : (s + 1) * 128]

    publish(1, acc2)
    own_sums = lane_sums(own_acc[...])

    drain(stage1.at[0, pl.ds(0, GROUPS - 1)], recv1.at[0])
    drain(stage1.at[1, pl.ds(0, GROUPS - 1)], recv1.at[1])
    for member in range(4):
        meet(met1, acc1, None, member)

    publish(0, acc1)
    for i in range(1, 8):
        th, te = (h + i // 2) % 4, (e + i) % 2
        remote(
            col_out.at[te], col_line.at[2 * h + e], col_send.at[0], col_recv.at[0], at(y, xx, th, te)
        ).start()
    col_line[2 * h + e] = col_out[e]
    siblings = []
    for i in (1, 2, 3):
        member = (grp + i) % 4
        copy = remote(
            row_acc.at[member], row_in.at[i - 1], row_send.at[i - 1], row_recv.at[i - 1], (blk, member)
        )
        copy.start()
        siblings.append(copy)
    drain(col_line.at[pl.ds(0, 7)], col_recv.at[0])

    def give(k):
        ty, tx = (y + k // 4) % 4, (xx + k % 4) % 4
        other_blk = ty * 16 + tx * 4 + h
        for u, a in ((0, back[other_blk]), (1, partners[2, other_blk])):
            for i in range(2):
                col_stage[k, u, i] = col_line[2 * (a % 4) + i, u]
        return ty, tx

    def give_peer(k):
        ty, tx = give(k)
        remote(
            col_stage.at[k], col_plane.at[y * 4 + xx], col_send.at[1], col_recv.at[1], at(ty, tx, h)
        ).start()

    for k in range(1, 16):
        give_peer(k)
    give(0)
    col_plane[y * 4 + xx] = col_stage[0]
    for copy in siblings:
        copy.wait()
    total = row_acc[grp] + row_in[0] + row_in[1] + row_in[2]
    density = jnp.sum(total, axis=0, keepdims=True) + own_sums
    drain(col_plane.at[pl.ds(0, 15)], col_recv.at[1])
    silent = jnp.logical_not(receives(blk))

    def column_sums(a, u, q):
        d = (a % 4 - q + 4) % 4
        j0 = jnp.where(d == 2, 3, jnp.where(d == 3, 2, d))
        j1 = jnp.where(d == 0, 2, jnp.where(d == 3, 3, d - 1))
        j = jnp.where(e == 0, j0, j1)
        return col_plane[a // 4, u, j // 2, pl.ds(j % 2, 1), :]

    for q in range(4):
        part = density[:, q * 128 : (q + 1) * 128] + column_sums(back[blk], 0, q)
        part = part + jnp.where(silent, column_sums(partners[2, blk], 1, q), 0.0)
        out[pl.ds(q, 1), :] = part

    for part in range(2):
        drain(pieces[part].at[pl.ds(0, GROUPS - 1)], spread_send.at[part])
        drain(stage1.at[part, pl.ds(0, GROUPS - 1)], send1.at[part])
    drain(stage2.at[pl.ds(0, GROUPS - 1)], send2)
    drain(col_line.at[pl.ds(0, 7)], col_send.at[0])
    drain(col_plane.at[pl.ds(0, 15)], col_send.at[1])


def body(embeddings, partners):
    f32, bf16, dma = jnp.float32, jnp.bfloat16, pltpu.SemaphoreType.DMA
    regular = pltpu.SemaphoreType.REGULAR
    density = pl.pallas_call(
        kernel,
        out_shape=jax.ShapeDtypeStruct((4, 128), f32),
        in_specs=[
            pl.BlockSpec(memory_space=pl.ANY),
            pl.BlockSpec(memory_space=pl.ANY),
        ],
        out_specs=pl.BlockSpec(memory_space=pltpu.VMEM),
        scratch_shapes=[
            pltpu.VMEM((4, ROWS, WIDTH), bf16),
            pltpu.VMEM((GROUPS, 16, 256), bf16),
            pltpu.VMEM((GROUPS, 16, 256), bf16),
            pltpu.VMEM((2, GROUPS, 16, 256), bf16),
            pltpu.VMEM((GROUPS, 16, 256), bf16),
            pltpu.VMEM((ROWS, WIDTH), bf16),
            pltpu.VMEM((ROWS, WIDTH), bf16),
            pltpu.VMEM((ROWS, 128), f32),
            pltpu.VMEM((ROWS, 128), f32),
            pltpu.VMEM((ROWS, 128), f32),
            pltpu.VMEM((4, 8, ROWS), f32),
            pltpu.VMEM((3, 8, ROWS), f32),
            pltpu.VMEM((2, 2, 2, 128), f32),
            pltpu.VMEM((8, 2, 2, 128), f32),
            pltpu.VMEM((16, 2, 2, 2, 128), f32),
            pltpu.VMEM((16, 2, 2, 2, 128), f32),
            pltpu.SMEM((3, GROUPS), jnp.int32),
            pltpu.SMEM((2, GROUPS), jnp.int32),
            pltpu.SMEM((GROUPS,), jnp.int32),
            pltpu.SMEM((2, GROUPS), jnp.int32),
            pltpu.SMEM((GROUPS,), jnp.int32),
            pltpu.SMEM((GROUPS,), jnp.int32),
            pltpu.SMEM((GROUPS,), jnp.int32),
            pltpu.SMEM((GROUPS,), jnp.int32),
            regular, regular, regular, regular,
            dma((2,)), dma((2,)), dma((2,)), dma((2,)), dma, dma,
            dma, dma, dma((4,)), dma((4,)), dma((2,)), dma((2,)), dma((3,)), dma((3,)), dma((2,)), dma((2,)),
        ],
        compiler_params=pltpu.CompilerParams(
            collective_id=0, has_side_effects=True, vmem_limit_bytes=60 * 2**20
        ),
        cost_estimate=pl.CostEstimate(
            flops=2 * 4 * ROWS * 3 * ROWS * WIDTH, bytes_accessed=2**20, transcendentals=12 * ROWS * ROWS
        ),
    )(partners, embeddings)
    return density.reshape(ROWS)


def solution(mesh):
    return jax.shard_map(
        body,
        mesh=mesh,
        in_specs=(P(("blk", "grp"), None), P()),
        out_specs=P(("blk", "grp")),
        check_vma=False,
    )
```

```python
import math

import jax
import jax.numpy as jnp
from jax import lax
from jax.experimental import pallas as pl
from jax.experimental.pallas import tpu as pltpu
from jax.sharding import PartitionSpec as P

MESH = pl.DeviceIdType.MESH
HEAT = 0.05
RATE = math.log2(math.e) / HEAT
GROUPS = 64
ROWS = 512
WIDTH = 1024
TILE = 256
EARLY = 64
PACE = ((7, 16), (21, 16))


def similarity(columns, members):
    c = lax.dot_general(columns, members, (((1,), (1,)), ((), ())), preferred_element_type=jnp.float32)
    return jnp.exp2(c * RATE - RATE)


def half_scores(columns, members, part):
    c = jnp.zeros((), jnp.float32)
    for i in range(2):
        k = slice(i * 512 + part * 256, i * 512 + part * 256 + 256)
        c = c + lax.dot_general(
            columns[:, i * 256 : i * 256 + 256], members[:, k], (((1,), (1,)), ((), ())), preferred_element_type=jnp.float32
        )
    return c


def lane_sums(total):
    parts = [jnp.sum(total[s * 128 : (s + 1) * 128].T, axis=0, keepdims=True) for s in range(4)]
    return jnp.concatenate(parts, axis=1)


def kernel(
    rounds, rows, out,
    own, pieces_a, pieces_b, stage1, stage2, met1_a, met1_b, scores, met2, own_acc, acc1, acc2, row_acc, row_in, col_out, col_line, col_stage, col_plane,
    partners, hop_a, low_a, hop_b, low_b, pick1, pick2, back,
    line_y, line_h, line_z, other, spread_send, spread_recv, send1, recv1, send2, recv2,
    load, table, own_send, own_recv, fwd_send, fwd_recv, row_send, row_recv, col_send, col_recv,
):
    blk, grp = lax.axis_index("blk"), lax.axis_index("grp")
    pieces, met1s = (pieces_a, pieces_b), (met1_a, met1_b)
    y, xx, h = blk // 16, (blk // 4) % 4, blk % 4
    e, c = grp // 2, grp % 2

    def at(y_, x_, h_, e_=None, c_=None):
        e_ = e if e_ is None else e_
        c_ = c if c_ is None else c_
        return ((y_ % 4) * 16 + (x_ % 4) * 4 + h_ % 4, e_ * 2 + c_)

    def signal(sem, device):
        pl.semaphore_signal(sem, inc=1, device_id=device, device_id_type=MESH)

    def remote(src, dst, send, recv, device):
        return pltpu.make_async_remote_copy(
            src_ref=src, dst_ref=dst, send_sem=send, recv_sem=recv, device_id=device, device_id_type=MESH
        )

    def drain(ref, sem):
        pltpu.make_async_copy(ref, ref, sem).wait()

    x = own.at[grp]
    fetch = pltpu.make_async_copy(rows, x, load)
    fetch.start()
    fetch_table = pltpu.make_async_copy(rounds, partners, table)
    fetch_table.start()

    def spread(dy, dx, dh, part=0):
        ty, tx, th = (y + dy) % 4, (xx + dx) % 4, (h + dh) % 4
        row = pl.multiple_of((th * 8 + ty * 2 + tx // 2) * 16, 16)
        col = pl.multiple_of((tx % 2) * 512 + part * 256, 256)
        remote(
            x.at[pl.ds(row, 16), pl.ds(col, 256)],
            pieces[part].at[blk],
            spread_send.at[part],
            spread_recv.at[part],
            at(ty, tx, th),
        ).start()

    def spread_lines(j, carry):
        spread(1 + j // 3, 0, 1 + j % 3)
        spread(0, 1 + j // 3, 1 + j % 3)
        return carry

    def spread_plane(j, carry):
        spread(1 + j // 3, 1 + j % 3, 0)
        return carry

    def spread_rest(j, carry):
        spread(1 + j // 9, 1 + (j // 3) % 3, 1 + j % 3)
        return carry

    barrier = pltpu.get_barrier_semaphore()
    for i in (1, 2, 3):
        signal(barrier, at(y + i, xx, h))
        signal(barrier, at(y, xx + i, h))
        signal(barrier, at(y, xx, h + i))
    signal(barrier, at(y, xx, h, 1 - e))
    signal(barrier, at(y, xx, h, e, 1 - c))
    signal(barrier, at(y, xx, h, 1 - e, 1 - c))
    fetch.wait()
    pl.semaphore_wait(barrier, 12)
    for i in (1, 2, 3):
        signal(line_y, at(y + i, xx, h))
        signal(line_h, at(y, xx, h + i))

    def own_chip(i, start, size):
        part = own.at[grp, pl.ds(start, size)]
        return remote(part, part, own_send.at[1 + i], own_recv.at[1 + i], at(y, xx, h, 1 - e))

    own_chip(0, 0, EARLY).start()
    for i in (1, 2, 3):
        spread(0, 0, i)
        spread(i, 0, 0)
        spread(0, i, 0)
    pl.semaphore_wait(line_y, 3)
    for i in (1, 2, 3):
        signal(line_z, at(y, xx, h + i))
    pl.semaphore_wait(line_h, 3)
    lax.fori_loop(0, 9, spread_lines, 0)
    pl.semaphore_wait(line_z, 3)
    signal(other, at(y, xx, h, 1 - e))
    lax.fori_loop(0, 27, spread_rest, 0)
    lax.fori_loop(0, 9, spread_plane, 0)

    def spread_second(k, carry):
        spread(k // 16, (k // 4) % 4, k % 4, 1)
        return carry

    lax.fori_loop(1, GROUPS, spread_second, 0)
    own_core = remote(x, x, own_send.at[0], own_recv.at[0], at(y, xx, h, e, 1 - c))
    own_core.start()
    my_row = pl.multiple_of((h * 8 + y * 2 + xx // 2) * 16, 16)
    my_col = pl.multiple_of((xx % 2) * 512, 512)
    for part in range(2):
        lanes = pl.ds(pl.multiple_of(my_col + part * 256, 256), 256)
        pieces[part][blk] = x[pl.ds(my_row, 16), lanes]

    def mate(g):
        return g + 4 - 8 * ((g // 4) % 2)

    def begin(g, carry):
        hop_a[0, g] = partners[1, partners[0, g]]
        hop_b[0, g] = mate(partners[2, g])
        low_a[g] = g
        low_b[g] = g
        return carry

    fetch_table.wait()
    lax.fori_loop(0, GROUPS, begin, 0)
    for step in range(5):
        now, later = step % 2, (step + 1) % 2

        def double(g, carry):
            s, t = hop_a[now, g], hop_b[now, g]
            low_a[g] = jnp.minimum(low_a[g], low_a[s])
            low_b[g] = jnp.minimum(low_b[g], low_b[t])
            hop_a[later, g] = hop_a[now, s]
            hop_b[later, g] = hop_b[now, t]
            return carry

        lax.fori_loop(0, GROUPS, double, 0)

    def first(g):
        return low_a[g] < low_a[partners[0, g]]

    def receives(g):
        return low_b[g] < low_b[partners[2, g]]

    def choose(g, carry):
        pick1[g] = jnp.where(first(g), partners[0, g], partners[1, g])
        back[g] = jnp.where(first(g), partners[1, g], partners[0, g])
        pick2[g] = partners[2, jnp.where(receives(g), g, mate(g))]
        return carry

    lax.fori_loop(0, GROUPS, choose, 0)

    own_acc[...] = jnp.zeros_like(own_acc)
    diagonal = lax.broadcasted_iota(jnp.int32, (ROWS, TILE), 0)
    across = lax.broadcasted_iota(jnp.int32, (ROWS, TILE), 1)

    for t in range(ROWS // TILE):
        terms = similarity(x[...], x[t * TILE : (t + 1) * TILE, :])
        terms = jnp.where(diagonal == across + t * TILE, 0.0, terms)
        own_acc[...] += terms[:, :128] + terms[:, 128:]

    def own_others(member):
        for t in range(ROWS // TILE):
            terms = similarity(x[...], own[member, t * TILE : (t + 1) * TILE, :])
            own_acc[...] += terms[:, :128] + terms[:, 128:]

    own_core.wait()
    own_others(e * 2 + 1 - c)

    def place(k):
        d = k % 4
        ty, tx, th = (y + k // 16) % 4, (xx + (k // 4) % 4) % 4, (h + k) % 4
        to = jnp.where(d == 0, e, jnp.where(d == 1, 0, jnp.where(d == 3, 1, 1 - e)))
        second0 = jnp.where(e == 0, d, d - 1)
        second1 = jnp.where(e == 0, 3 - d, jnp.where(d == 0, 0, 1))
        slot = 2 * e + jnp.where(to == 0, second0, second1)
        row = pl.multiple_of(slot * 128 + (y * 2 + xx // 2) * 16, 16)
        return ty, tx, th, to, row

    half = pl.multiple_of((xx % 2) * 256, 256)
    home = pl.multiple_of((2 * e + 0) * 128 + (y * 2 + xx // 2) * 16, 16)

    def half_units(part):
        def send(j, carry):
            k = (j // 8) * 16 + (2 * ((j // 4) % 2) + (part + xx) % 2) * 4 + j % 4
            ty, tx, th, to, row = place(k)
            stage2[k] = pieces[part][pick2[ty * 16 + tx * 4 + th]]
            col = pl.multiple_of((xx % 2) * 512 + part * 256, 256)
            remote(
                stage2.at[k], met2.at[pl.ds(row, 16), pl.ds(col, 256)], send2, recv2, at(ty, tx, th, to)
            ).start()
            return carry

        lax.fori_loop(1 - (part + xx) % 2, GROUPS // 2, send, 0)

    def units(part, first_row):
        count, size = PACE[part]
        per = (GROUPS - 1) // count

        def send(k, carry):
            ty, tx, th, to, row = place(k)
            stage1[part, k] = pieces[part][pick1[ty * 16 + tx * 4 + th]]
            remote(
                stage1.at[part, k],
                met1s[part].at[pl.ds(row, 16), pl.ds(half, 256)],
                send1.at[part],
                recv1.at[part],
                at(ty, tx, th, to),
            ).start()
            return carry

        def group(i, carry):
            own_chip(1, pl.multiple_of(first_row + i * size, 16), size).start()
            return lax.fori_loop(1 + i * per, 1 + (i + 1) * per, send, carry)

        lax.fori_loop(0, count, group, 0)
        lax.fori_loop(1 + count * per, GROUPS, send, 0)
        met1s[part][pl.ds(home, 16), pl.ds(half, 256)] = pieces[part][pick1[blk]]

    drain(pieces_a.at[pl.ds(0, GROUPS - 1)], spread_recv.at[0])
    pl.semaphore_wait(other, 1)
    half_units(0)
    drain(pieces_b.at[pl.ds(0, GROUPS - 1)], spread_recv.at[1])
    half_units(1)
    units(0, EARLY)
    units(1, EARLY + PACE[0][0] * PACE[0][1])
    met2[pl.ds(home, 16), pl.ds(pl.multiple_of(my_col + half, 256), 256)] = jnp.where(
        xx % 2 == 0, pieces_a[pick2[blk]], pieces_b[pick2[blk]]
    )

    def meet(met, acc, counts, member):
        for t in range(ROWS // TILE):
            part = slice(t * TILE, (t + 1) * TILE)
            terms = similarity(met[...], own[member, part, :])
            acc[...] += terms[:, :128] + terms[:, 128:]
            sums = jnp.sum(terms.reshape(ROWS // 8, 8, TILE), axis=0)
            if counts is not None:
                row_acc[member, :, part] = jnp.where(counts, sums, 0.0)
            else:
                row_acc[member, :, part] += sums

    drain(stage2.at[pl.ds(0, GROUPS - 1)], recv2)
    pair = at(y, xx + 1 - 2 * (xx % 2), h)
    for i in range(2):
        columns = pl.ds(pl.multiple_of(i * 512 + half, 256), 256)
        remote(met2.at[:, columns], met2.at[:, columns], fwd_send.at[i], fwd_recv.at[i], pair).start()
    acc1[...] = jnp.zeros_like(acc1)
    acc2[...] = jnp.zeros_like(acc2)
    for i in range(2):
        columns = pl.ds(pl.multiple_of(i * 512 + half, 256), 256)
        remote(met2.at[:, columns], met2.at[:, columns], fwd_send.at[i], fwd_recv.at[i], pair).wait()
    counts = receives(blk)
    meet(met2, acc2, counts, grp)
    meet(met2, acc2, counts, 2 * e + 1 - c)
    own_chip(0, 0, EARLY).wait()
    own_chip(1, EARLY, ROWS - EARLY).wait()
    across_core = remote(
        own.at[2 - 2 * e + c], own.at[2 - 2 * e + c], own_send.at[3], own_recv.at[3], at(y, xx, h, e, 1 - c)
    )
    across_core.start()
    own_others(2 - 2 * e + c)
    meet(met2, acc2, counts, 2 - 2 * e + c)
    across_core.wait()
    own_others(2 - 2 * e + 1 - c)
    meet(met2, acc2, counts, 2 - 2 * e + 1 - c)

    def publish(u, acc):
        sums = lane_sums(acc[...])
        for s in range(4):
            col_out[s // 2, u, pl.ds(s % 2, 1), :] = sums[:, s * 128 : (s + 1) * 128]

    publish(1, acc2)
    own_sums = lane_sums(own_acc[...])

    drain(stage1.at[0, pl.ds(0, GROUPS - 1)], recv1.at[0])
    for t in range(8):
        member, part = t // 2, slice((t % 2) * TILE, (t % 2 + 1) * TILE)
        scores[t] = half_scores(met1_a[...], own[member, part, :], 0)
    drain(stage1.at[1, pl.ds(0, GROUPS - 1)], recv1.at[1])
    for t in range(8):
        member, part = t // 2, slice((t % 2) * TILE, (t % 2 + 1) * TILE)
        terms = jnp.exp2((scores[t] + half_scores(met1_b[...], own[member, part, :], 1)) * RATE - RATE)
        acc1[...] += terms[:, :128] + terms[:, 128:]
        row_acc[member, :, part] += jnp.sum(terms.reshape(ROWS // 8, 8, TILE), axis=0)

    publish(0, acc1)
    for i in range(1, 8):
        th, te = (h + i // 2) % 4, (e + i) % 2
        remote(
            col_out.at[te], col_line.at[2 * h + e], col_send.at[0], col_recv.at[0], at(y, xx, th, te)
        ).start()
    col_line[2 * h + e] = col_out[e]
    siblings = []
    for i in (1, 2, 3):
        member = (grp + i) % 4
        copy = remote(
            row_acc.at[member], row_in.at[i - 1], row_send.at[i - 1], row_recv.at[i - 1], (blk, member)
        )
        copy.start()
        siblings.append(copy)
    drain(col_line.at[pl.ds(0, 7)], col_recv.at[0])

    def give(k):
        ty, tx = (y + k // 4) % 4, (xx + k % 4) % 4
        other_blk = ty * 16 + tx * 4 + h
        for u, a in ((0, back[other_blk]), (1, partners[2, other_blk])):
            for i in range(2):
                col_stage[k, u, i] = col_line[2 * (a % 4) + i, u]
        return ty, tx

    def give_peer(k):
        ty, tx = give(k)
        remote(
            col_stage.at[k], col_plane.at[y * 4 + xx], col_send.at[1], col_recv.at[1], at(ty, tx, h)
        ).start()

    for k in range(1, 16):
        give_peer(k)
    give(0)
    col_plane[y * 4 + xx] = col_stage[0]
    for copy in siblings:
        copy.wait()
    total = row_acc[grp] + row_in[0] + row_in[1] + row_in[2]
    density = jnp.sum(total, axis=0, keepdims=True) + own_sums
    drain(col_plane.at[pl.ds(0, 15)], col_recv.at[1])
    silent = jnp.logical_not(receives(blk))

    def column_sums(a, u, q):
        d = (a % 4 - q + 4) % 4
        j0 = jnp.where(d == 2, 3, jnp.where(d == 3, 2, d))
        j1 = jnp.where(d == 0, 2, jnp.where(d == 3, 3, d - 1))
        j = jnp.where(e == 0, j0, j1)
        return col_plane[a // 4, u, j // 2, pl.ds(j % 2, 1), :]

    for q in range(4):
        part = density[:, q * 128 : (q + 1) * 128] + column_sums(back[blk], 0, q)
        part = part + jnp.where(silent, column_sums(partners[2, blk], 1, q), 0.0)
        out[pl.ds(q, 1), :] = part

    for part in range(2):
        drain(pieces[part].at[pl.ds(0, GROUPS - 1)], spread_send.at[part])
        drain(stage1.at[part, pl.ds(0, GROUPS - 1)], send1.at[part])
    drain(stage2.at[pl.ds(0, GROUPS - 1)], send2)
    drain(col_line.at[pl.ds(0, 7)], col_send.at[0])
    drain(col_plane.at[pl.ds(0, 15)], col_send.at[1])


def body(embeddings, partners):
    f32, bf16, dma = jnp.float32, jnp.bfloat16, pltpu.SemaphoreType.DMA
    regular = pltpu.SemaphoreType.REGULAR
    density = pl.pallas_call(
        kernel,
        out_shape=jax.ShapeDtypeStruct((4, 128), f32),
        in_specs=[
            pl.BlockSpec(memory_space=pl.ANY),
            pl.BlockSpec(memory_space=pl.ANY),
        ],
        out_specs=pl.BlockSpec(memory_space=pltpu.VMEM),
        scratch_shapes=[
            pltpu.VMEM((4, ROWS, WIDTH), bf16),
            pltpu.VMEM((GROUPS, 16, 256), bf16),
            pltpu.VMEM((GROUPS, 16, 256), bf16),
            pltpu.VMEM((2, GROUPS, 16, 256), bf16),
            pltpu.VMEM((GROUPS, 16, 256), bf16),
            pltpu.VMEM((ROWS, WIDTH // 2), bf16),
            pltpu.VMEM((ROWS, WIDTH // 2), bf16),
            pltpu.VMEM((8, ROWS, TILE), f32),
            pltpu.VMEM((ROWS, WIDTH), bf16),
            pltpu.VMEM((ROWS, 128), f32),
            pltpu.VMEM((ROWS, 128), f32),
            pltpu.VMEM((ROWS, 128), f32),
            pltpu.VMEM((4, 8, ROWS), f32),
            pltpu.VMEM((3, 8, ROWS), f32),
            pltpu.VMEM((2, 2, 2, 128), f32),
            pltpu.VMEM((8, 2, 2, 128), f32),
            pltpu.VMEM((16, 2, 2, 2, 128), f32),
            pltpu.VMEM((16, 2, 2, 2, 128), f32),
            pltpu.SMEM((3, GROUPS), jnp.int32),
            pltpu.SMEM((2, GROUPS), jnp.int32),
            pltpu.SMEM((GROUPS,), jnp.int32),
            pltpu.SMEM((2, GROUPS), jnp.int32),
            pltpu.SMEM((GROUPS,), jnp.int32),
            pltpu.SMEM((GROUPS,), jnp.int32),
            pltpu.SMEM((GROUPS,), jnp.int32),
            pltpu.SMEM((GROUPS,), jnp.int32),
            regular, regular, regular, regular,
            dma((2,)), dma((2,)), dma((2,)), dma((2,)), dma, dma,
            dma, dma, dma((4,)), dma((4,)), dma((2,)), dma((2,)), dma((3,)), dma((3,)), dma((2,)), dma((2,)),
        ],
        compiler_params=pltpu.CompilerParams(
            collective_id=0, has_side_effects=True, vmem_limit_bytes=60 * 2**20
        ),
        cost_estimate=pl.CostEstimate(
            flops=2 * 4 * ROWS * 3 * ROWS * WIDTH, bytes_accessed=2**20, transcendentals=12 * ROWS * ROWS
        ),
    )(partners, embeddings)
    return density.reshape(ROWS)


def solution(mesh):
    return jax.shard_map(
        body,
        mesh=mesh,
        in_specs=(P(("blk", "grp"), None), P()),
        out_specs=P(("blk", "grp")),
        check_vma=False,
    )
```
